256 devices in a mesh: row: 32 (over z, x), col: 8 (over y, core).
Axes of the slice: x: 4, y: 4, z: 8, core: 2. Of those that a mesh axis runs over, the one named last changes fastest.
Arguments:
- gate_pre: bfloat16 [4096, 16384], P('col', 'row'), may hold values from -6 to 6
- up_pre: bfloat16 [4096, 16384], P('col', 'row'), may hold values from -6 to 6
- weight: bfloat16 [16384, 8192], P('row', 'col'), may hold values from -0.0625 to 0.0625
- block_mask: int32 [128, 64], P('row', 'col'), may hold values from 0 to 1, as said below
- grad_out: bfloat16 [4096, 8192], P('row', 'col'), may hold values from -6 to 6
Outputs:
- output: bfloat16 [4096, 8192], P('row', 'col')
- grad_gate: bfloat16 [4096, 16384], P('col', 'row')
- grad_up: bfloat16 [4096, 16384], P('col', 'row')
- grad_weight: bfloat16 [16384, 8192], P('row', 'col')
The draws below stay inside these ranges and needn't reach their ends.
Inputs may be any that keep to these rules, and one draw needn't show every extreme that they name: `block_mask`: exactly half of the blocks are kept; block rows 2m and 2m + 1 together keep 64 blocks, each of them between 8 and 56 blocks.
All inputs are finite; a program needn't handle non-finite values.
Results may differ from the reference program's by a relative error of at most 0.02.
Values may be sent and summed in bfloat16 or wider, within the bound.
A program may use at most 320 MiB of HBM per device.

```python
import jax
import jax.numpy as jnp
from jax import lax

D = 8192
FF = 16384
BLOCK = 128
TOKENS = 4096
FB = 128
DB = 64
N_ROW = 32


def draw_block_mask(key, part):
    key = jax.random.fold_in(key, 7)
    count_key, order_key = jax.random.split(key)
    lowest = DB // 8
    first = jax.random.randint(count_key, (FB // 2,), lowest, DB - lowest + 1)
    counts = jnp.stack([first, DB - first], axis=1).reshape(FB)
    ranks = jax.vmap(lambda k: jax.random.permutation(k, DB))(jax.random.split(order_key, FB))
    return (ranks < counts[:, None]).astype(jnp.int32)


def spiked(array, stream_key, source, target, shards_of, factor):
    owner, partner = [(jnp.arange(array.shape[position]) // (array.shape[position] // shards_of)).reshape([-1 if axis == position else 1 for axis in range(array.ndim)]) for position in (source, target)]
    chosen = jax.random.permutation(stream_key, shards_of)[partner]
    strong = (owner == chosen) | (owner == (partner + shards_of // 2) % shards_of)
    return jnp.where(strong, factor * array, array)


def level_of(stream_key, extent, cuts, smallest, largest):
    gain = 1.0
    for position, parts in cuts:
        steps = jax.random.uniform(jax.random.fold_in(jax.random.fold_in(stream_key, 6), position), (parts,), jnp.float32, smallest / len(cuts), largest / len(cuts))
        gain = gain * jnp.repeat(jnp.exp(steps), extent[position] // parts).reshape((-1,) + (1,) * (len(extent) - 1 - position))
    return gain


def normal_values(rng, extent, deviation, bound, shards=(), dtype=jnp.bfloat16):
    entries = deviation * jax.random.normal(rng, extent, jnp.float32)
    if shards:
        entries = entries * level_of(rng, extent, shards, -0.22, 0.18)
    return jnp.clip(entries, -bound, bound).astype(dtype)


def heavy_noise(rng, extent, scale, bound, cuts, heavy, dtype=jnp.bfloat16):
    array = scale * jax.random.normal(rng, extent, jnp.float32)
    if cuts:
        array = array * level_of(rng, extent, cuts, -0.22, 0.18)
    return jnp.clip(spiked(array, jax.random.fold_in(rng, 3), *heavy), -bound, bound).astype(dtype)


def setup_inputs(seed: int = 0) -> dict:
    streams_of = jax.random.split(jax.random.key(seed), 6)
    gate_pre = normal_values(streams_of[0], (TOKENS, FF), 1.5, 6.0, ((0, 8), (1, 32)))
    up_pre = heavy_noise(streams_of[1], (TOKENS, FF), 1.0, 6.0, ((0, 8), (1, 32)), (1, 0, 32, 2.75))
    weight = normal_values(streams_of[2], (FF, D), (FF // 2) ** -0.5, 0.0625, ((0, 32), (1, 8)))
    block_mask = draw_block_mask(jax.random.fold_in(streams_of[5], 71), 0)
    grad_out = heavy_noise(streams_of[4], (TOKENS, D), 1.0, 6.0, ((0, 32), (1, 8)), (1, 0, 32, 2.75))
    return {"gate_pre": gate_pre, "up_pre": up_pre, "weight": weight, "block_mask": block_mask, "grad_out": grad_out}


def reference(gate_pre, up_pre, weight, block_mask, grad_out):
    keep = jnp.repeat(jnp.repeat(block_mask, BLOCK, 0), BLOCK, 1).astype(jnp.bfloat16)
    masked = weight * keep
    gate32 = gate_pre.astype(jnp.float32)
    up32 = up_pre.astype(jnp.float32)
    sig = jax.nn.sigmoid(gate32)
    hidden = (gate32 * sig * up32).astype(jnp.bfloat16)
    width = FF // N_ROW

    def add_part(index, total):
        start = (index * width).astype(jnp.int32)
        left = lax.dynamic_slice_in_dim(hidden, start, width, 1)
        right = lax.dynamic_slice_in_dim(masked, start, width, 0)
        part = jnp.dot(left, right, preferred_element_type=jnp.float32).astype(jnp.bfloat16)
        part = lax.optimization_barrier(part)
        return total + part.astype(jnp.float32)

    output = lax.fori_loop(0, N_ROW, add_part, jnp.zeros((TOKENS, D), jnp.float32)).astype(jnp.bfloat16)
    grad_hidden = lax.dot_general(grad_out, masked, (((1,), (1,)), ((), ())), preferred_element_type=jnp.float32)
    grad_up = (grad_hidden * gate32 * sig).astype(jnp.bfloat16)
    grad_gate = (grad_hidden * up32 * sig * (1.0 + gate32 * (1.0 - sig))).astype(jnp.bfloat16)
    product = lax.dot_general(hidden, grad_out, (((0,), (0,)), ((), ())), preferred_element_type=jnp.float32)
    grad_weight = (product * keep.astype(jnp.float32)).astype(jnp.bfloat16)
    return output, grad_gate, grad_up, grad_weight
```

```python
import jax
import jax.numpy as jnp
from jax import lax
from jax.experimental import pallas as pl
from jax.experimental.pallas import tpu as pltpu
from jax.sharding import PartitionSpec as P

NZ, NX, NY = 8, 4, 4
SHARD = 128
CUT = 80
REST = SHARD - CUT
MESH = pl.DeviceIdType.MESH
F32 = jnp.float32
BF16 = jnp.bfloat16
ORDER = (4, 3, -3, 2, -2, 1, -1, 0)


class Slots:
    def __init__(self):
        self.known = {}

    def __call__(self, *key):
        return self.known.setdefault(key, len(self.known))


def kernel(
    grad_ref, gate_ref, up_ref, weight_ref, mask_ref,
    out_ref, dgate_ref, dup_ref, dweight_ref,
    gall, hall, part, wm, dpart, acc,
    land_a, land_b, land_s, land_y,
    send_sem, recv_sem,
):
    row, col = lax.axis_index("row"), lax.axis_index("col")
    z, x = row // NX, row % NX
    y, core = col // 2, col % 2

    def zi(o):
        return lax.rem(z + (o + NZ), NZ)

    def xi(d):
        return lax.rem(x + (d + NX), NX)

    def yi(d):
        return lax.rem(y + (d + NY), NY)

    def zdev(d):
        return (zi(d) * NX + x, col)

    def xdev(d):
        return (z * NX + xi(d), col)

    def ydev(d):
        return (row, yi(d) * 2 + core)

    sibling = (row, y * 2 + (1 - core))

    sems, slot_a, slot_b = Slots(), Slots(), Slots()
    sends = []

    def send(src, dst, dev, *key):
        copy = pltpu.make_async_remote_copy(
            src_ref=src, dst_ref=dst, send_sem=send_sem.at[len(sends)],
            recv_sem=recv_sem.at[sems(*key)], device_id=dev, device_id_type=MESH,
        )
        copy.start()
        sends.append(copy)

    def arrive(dst, *key):
        pltpu.make_async_remote_copy(
            src_ref=dst, dst_ref=dst, send_sem=send_sem.at[0],
            recv_sem=recv_sem.at[sems(*key)], device_id=sibling, device_id_type=MESH,
        ).wait_recv()

    def add(dst, rows, *terms):
        @pl.loop(0, rows // 16)
        def _(i):
            at = pl.ds(pl.multiple_of(i * 16, 16), 16)
            total = terms[0].at[at, :][...].astype(F32)
            for term in terms[1:]:
                total = total + term.at[at, :][...].astype(F32)
            dst.at[at, :][...] = total.astype(BF16)

    barrier = pltpu.get_barrier_semaphore()
    for dev in (zdev(1), zdev(-1), xdev(1), xdev(-1), ydev(1), ydev(-1), sibling):
        pl.semaphore_signal(barrier, inc=1, device_id=dev, device_id_type=MESH)

    own_rows = pl.ds(pl.multiple_of(x * SHARD, SHARD), SHARD)

    @pl.loop(0, SHARD // 16)
    def _(i):
        at = pl.ds(pl.multiple_of(i * 16, 16), 16)
        gall[z, pl.ds(pl.multiple_of(x * SHARD + i * 16, 16), 16), :] = grad_ref[at, :]

    @pl.loop(0, 16)
    def _(i):
        at = pl.ds(pl.multiple_of(i * 32, 32), 32)
        g = gate_ref[at, :].astype(F32)
        u = up_ref[at, :].astype(F32)
        hall[col, at, :] = (g * jax.nn.sigmoid(g) * u).astype(BF16)

    pl.semaphore_wait(barrier, 7)

    def rows_a(buf, o, d):
        return buf.at[zi(o), pl.ds(pl.multiple_of(xi(d) * SHARD, 16), CUT), :]

    def rows_b(buf, o, d):
        return buf.at[zi(o), pl.ds(pl.multiple_of(xi(d) * SHARD + CUT, 16), REST), :]

    def ga(o, d):
        return rows_a(gall, o, d)

    def gb(o, d):
        return rows_b(gall, o, d)

    def hid(dy, h=None):
        at = slice(None) if h is None else pl.ds(h * 256, 256)
        return hall.at[yi(dy) * 2 + core, at, :]

    def hid_sibling(dy):
        return hall.at[yi(dy) * 2 + (1 - core)]

    def az_next(o):
        if o <= 0 and o > -4:
            send(ga(o, 0), ga(o, 0), zdev(1), "gaz", o - 1)
        if o >= 0 and o < 3:
            send(ga(o, 0), ga(o, 0), zdev(-1), "gaz", o + 1)

    def ax_first(o):
        send(ga(o, 0), ga(o, 0), xdev(1), "gax", o, -1)
        send(ga(o, 0), ga(o, 0), xdev(-1), "gax", o, 1)

    def az(o):
        arrive(ga(o, 0), "gaz", o)
        az_next(o)
        ax_first(o)

    def ax1(o):
        via = 1 if o % 2 == 0 else -1
        for d in (-via, via):
            arrive(ga(o, d), "gax", o, d)
            if d == -via:
                send(ga(o, d), ga(o, d), xdev(via), "gax", o, 2)

    def ax2(o):
        arrive(ga(o, 2), "gax", o, 2)

    def bz_first(d):
        send(gb(0, d), gb(0, d), zdev(1), "gbz", d, -1)
        send(gb(0, d), gb(0, d), zdev(-1), "gbz", d, 1)

    def bx(d):
        arrive(gb(0, d), "gbx", d)
        if d == -1:
            send(gb(0, d), gb(0, d), xdev(1), "gbx", 2)
        bz_first(d)

    def bz(o, d):
        low, high = (-4, 3) if d % 2 == 0 else (-3, 4)
        if o < low or o > high:
            return
        arrive(gb(o, d), "gbz", d, o)
        if o < 0 and o > low:
            send(gb(o, d), gb(o, d), zdev(1), "gbz", d, o - 1)
        if o > 0 and o < high:
            send(gb(o, d), gb(o, d), zdev(-1), "gbz", d, o + 1)

    def bz_all(k):
        for d in (0, -1, 1, 2):
            bz(-k, d)
            bz(k, d)

    def h0():
        for h in (0, 1):
            send(hid(0, h), hid(0, h), ydev(1), "hy", -1, h)
            send(hid(0, 1 - h), hid(0, 1 - h), ydev(-1), "hy", 1, 1 - h)
        send(hid(0), hid(0), sibling, "hs", 0)

    def h1():
        arrive(hid(-1, 0), "hy", -1, 0)
        send(hid(-1, 0), hid(-1, 0), ydev(1), "hy2", 0)
        arrive(hid(1, 1), "hy", 1, 1)
        send(hid(1, 1), hid(1, 1), ydev(-1), "hy2", 1)

    def h2():
        arrive(hid(-1, 1), "hy", -1, 1)
        send(hid(-1), hid(-1), sibling, "hs", -1)
        arrive(hid(1, 0), "hy", 1, 0)
        send(hid(1), hid(1), sibling, "hs", 1)

    def h3():
        arrive(hid(2, 0), "hy2", 0)
        arrive(hid(2, 1), "hy2", 1)
        send(hid(2), hid(2), sibling, "hs", 2)

    def h4():
        for dy in (0, -1, 1, 2):
            arrive(hid_sibling(dy), "hs", dy)

    def mm_part(o):
        block = zi(o)

        @pl.loop(0, 4)
        def _(n):
            at = pl.ds(pl.multiple_of(n * 256, 256), 256)
            part[block, :, at] = jnp.dot(hall[block], wm[:, at], preferred_element_type=F32).astype(BF16)

    def mm_dpart(block):
        @pl.loop(0, 2)
        def _(n):
            at = pl.ds(pl.multiple_of(n * 256, 256), 256)
            dpart[block, :, at] = lax.dot_general(
                gall[block], wm[at, :], (((1,), (1,)), ((), ())), preferred_element_type=F32
            ).astype(BF16)

    def mm_weight(block, first):
        @pl.loop(0, 4)
        def _(n):
            at = pl.ds(pl.multiple_of(n * 256, 256), 256)
            product = lax.dot_general(
                hall[block], gall[block, :, at], (((0,), (0,)), ((), ())), preferred_element_type=F32
            )
            acc[:, at] = product if first else acc[:, at] + product

    def pa(o, d):
        return rows_a(part, o, d)

    def pb(o, d):
        return rows_b(part, o, d)

    def la(*key):
        return land_a.at[slot_a(*key)]

    def lb(*key):
        return land_b.at[slot_b(*key)]

    def via_of(o):
        return 1 if o % 2 == 0 else -1

    def xs(o):
        via = via_of(o)
        send(pa(o, 2), la("pxm", o), xdev(via), "pxm", o)
        send(pa(o, -via), la("pxl", o, via), xdev(-via), "pxl", o, via)

    def xm(o):
        via = via_of(o)
        held = la("pxm", o)
        arrive(held, "pxm", o)
        add(held, CUT, held, pa(o, via))
        send(held, la("pxl", o, -via), xdev(via), "pxl", o, -via)

    def zf(o):
        sides = []
        if 0 <= o < 4:
            sides.append(-1)
        if -3 < o <= 0:
            sides.append(1)
        left, right = la("pxl", o, -1), la("pxl", o, 1)
        arrive(left, "pxl", o, -1)
        arrive(right, "pxl", o, 1)
        terms = [pa(o, 0), left, right]
        for side in sides:
            held = la("pz", o, side)
            arrive(held, "pz", o, side)
            terms.append(held)
        if o == 0:
            add(out_ref.at[pl.ds(0, CUT), :], CUT, *terms)
            return
        add(left, CUT, *terms)
        if o > 0:
            send(left, la("pz", o - 1, -1), zdev(1), "pz", o - 1, -1)
        else:
            send(left, la("pz", o + 1, 1), zdev(-1), "pz", o + 1, 1)

    def rz(o):
        for d in (0, -1, 1, 2):
            even = d % 2 == 0
            sides = []
            if 0 <= o < 4 and not (o == 3 and not even):
                sides.append(-1)
            if -4 < o <= 0 and not (o == -3 and even):
                sides.append(1)
            terms = [pb(o, d)]
            for side in sides:
                held = lb("pbz", d, o, side)
                arrive(held, "pbz", d, o, side)
                terms.append(held)
            src = terms[-1]
            if len(terms) > 1:
                add(src, REST, *terms)
            if o == 4:
                if even:
                    send(src, lb("pbz", d, 3, -1), zdev(1), "pbz", d, 3, -1)
                else:
                    send(src, lb("pbz", d, -3, 1), zdev(-1), "pbz", d, -3, 1)
            elif o > 0:
                send(src, lb("pbz", d, o - 1, -1), zdev(1), "pbz", d, o - 1, -1)
            elif o < 0:
                send(src, lb("pbz", d, o + 1, 1), zdev(-1), "pbz", d, o + 1, 1)

    def rsum(d):
        return lb("pbz", d, 0, 1)

    def bs():
        send(rsum(2), lb("pbxm"), xdev(1), "pbxm")
        send(rsum(-1), lb("pbxl", 1), xdev(-1), "pbxl", 1)

    def bm():
        held = lb("pbxm")
        arrive(held, "pbxm")
        add(held, REST, held, rsum(1))
        send(held, lb("pbxl", -1), xdev(1), "pbxl", -1)

    def bf():
        left, right = lb("pbxl", -1), lb("pbxl", 1)
        arrive(left, "pbxl", -1)
        arrive(right, "pbxl", 1)
        add(out_ref.at[pl.ds(CUT, REST), :], REST, rsum(0), left, right)

    def own(dy):
        return yi(dy) * 2 + core

    def dhalf(dy, h):
        return dpart.at[own(dy), pl.ds(h * 256, 256), :]

    S = {2: 0, -1: 1, 1: 2, 0: 3}
    Y = {("m", -1): 0, ("m", 1): 1, (-1, 0): 2, (-1, 1): 3, (1, 0): 4, (1, 1): 5}

    def ly(*key):
        return land_y.at[Y[key]]

    def ds_(dy):
        other = yi(dy) * 2 + (1 - core)
        mm_dpart(other)
        send(dpart.at[other], land_s.at[S[dy]], sibling, "ds", dy)
        mm_dpart(own(dy))

    def da(dy):
        held = land_s.at[S[dy]]
        arrive(held, "ds", dy)
        mine = dpart.at[own(dy)]
        add(mine, 512, mine, held)
        if dy == 2:
            send(dhalf(2, 0), ly("m", -1), ydev(1), "dym", -1)
            send(dhalf(2, 1), ly("m", 1), ydev(-1), "dym", 1)
        if dy == 1:
            send(dhalf(1, 1), ly(-1, 1), ydev(1), "dyf", -1, 1)
        if dy == -1:
            send(dhalf(-1, 0), ly(1, 0), ydev(-1), "dyf", 1, 0)

    def dm():
        for side, h in ((-1, 0), (1, 1)):
            held = ly("m", side)
            arrive(held, "dym", side)
            add(held, 256, held, dhalf(-side, h))
            send(held, ly(side, h), ydev(-side), "dyf", side, h)

    def df():
        for h in (1, 0):
            for side in (-1, 1):
                arrive(ly(side, h), "dyf", side, h)
        for h in (0, 1):
            @pl.loop(0, 8)
            def _(i):
                at = pl.ds(pl.multiple_of(i * 32, 32), 32)
                rows = pl.ds(pl.multiple_of(h * 256 + i * 32, 32), 32)
                dh = (
                    dhalf(0, h).at[at, :][...].astype(F32)
                    + ly(-1, h).at[at, :][...].astype(F32)
                    + ly(1, h).at[at, :][...].astype(F32)
                )
                g = gate_ref[rows, :].astype(F32)
                u = up_ref[rows, :].astype(F32)
                sig = jax.nn.sigmoid(g)
                dup_ref[rows, :] = (dh * g * sig).astype(BF16)
                dgate_ref[rows, :] = (dh * u * sig * (1.0 + g * (1.0 - sig))).astype(BF16)

    def mask_into(dst, src):
        @pl.loop(0, 4)
        def _(i):
            at = pl.ds(pl.multiple_of(i * 128, 128), 128)
            for j in range(8):
                cols = pl.ds(j * 128, 128)
                dst[at, cols] = (src[at, cols].astype(F32) * mask_ref[i, j].astype(F32)).astype(BF16)

    send(gb(0, 0), gb(0, 0), xdev(1), "gbx", -1)
    send(gb(0, 0), gb(0, 0), xdev(-1), "gbx", 1)
    az_next(0)
    ax_first(0)
    bz_first(0)
    h0()
    mask_into(wm, weight_ref)
    bx(-1)
    bx(1)
    az(-1)
    az(1)
    ax1(0)
    bx(2)
    h1()
    bz_all(1)
    az(-2)
    az(2)
    ax1(-1)
    ax1(1)
    h2()
    bz_all(2)
    h3()
    az(-3)
    az(3)
    ax1(-2)
    ax1(2)
    h4()
    mm_part(ORDER[0])
    bz_all(3)
    mm_part(ORDER[1])
    az(-4)
    ax1(-3)
    ax1(3)
    mm_part(ORDER[2])
    xs(ORDER[0])
    rz(ORDER[0])
    bz_all(4)
    mm_part(ORDER[3])
    ax1(-4)
    xs(ORDER[1])
    for o in (0, -1, 1, -2, 2, -3, 3, -4):
        ax2(o)

    def tick(t):
        if t + 1 < 8 and t >= 1:
            xs(ORDER[t + 1])
        if 1 <= t <= 8:
            xm(ORDER[t - 1])
        if 1 <= t <= 7:
            rz(ORDER[t])
        if 2 <= t <= 9:
            zf(ORDER[t - 2])
        if t + 4 < 8:
            mm_part(ORDER[t + 4])
        if t == 7:
            bs()
        if t == 8:
            bm()
        if t == 9:
            bf()

    def weight_piece(k):
        mm_weight(k, k == 0)

    tick(0)
    ds_(2)
    tick(1)
    ds_(-1)
    da(2)
    tick(2)
    ds_(1)
    da(-1)
    tick(3)
    ds_(0)
    da(1)
    tick(4)
    dm()
    da(0)
    weight_piece(0)
    tick(5)
    weight_piece(1)
    weight_piece(2)
    tick(6)
    weight_piece(3)
    weight_piece(4)
    tick(7)
    df()
    weight_piece(5)
    tick(8)
    weight_piece(6)
    weight_piece(7)
    mask_into(dweight_ref, acc)
    tick(9)

    for copy in sends:
        copy.wait_send()


def shards(gate_pre, up_pre, weight, block_mask, grad_out):
    vmem = pl.BlockSpec(memory_space=pltpu.VMEM)
    return pl.pallas_call(
        kernel,
        out_shape=(
            jax.ShapeDtypeStruct((SHARD, 1024), BF16),
            jax.ShapeDtypeStruct((512, 512), BF16),
            jax.ShapeDtypeStruct((512, 512), BF16),
            jax.ShapeDtypeStruct((512, 1024), BF16),
        ),
        in_specs=[vmem] * 4 + [pl.BlockSpec(memory_space=pltpu.SMEM)],
        out_specs=[vmem] * 4,
        scratch_shapes=[
            pltpu.VMEM((NZ, 512, 1024), BF16),
            pltpu.VMEM((8, 512, 512), BF16),
            pltpu.VMEM((NZ, 512, 1024), BF16),
            pltpu.VMEM((512, 1024), BF16),
            pltpu.VMEM((8, 512, 512), BF16),
            pltpu.VMEM((512, 1024), F32),
            pltpu.VMEM((31, CUT, 1024), BF16),
            pltpu.VMEM((31, REST, 1024), BF16),
            pltpu.VMEM((4, 512, 512), BF16),
            pltpu.VMEM((6, 256, 512), BF16),
            pltpu.SemaphoreType.DMA((144,)),
            pltpu.SemaphoreType.DMA((144,)),
        ],
        compiler_params=pltpu.CompilerParams(
            collective_id=0, has_side_effects=True, vmem_limit_bytes=58 * 2**20
        ),
        cost_estimate=pl.CostEstimate(flops=12 * 2**30, bytes_accessed=8 * 2**20, transcendentals=2**19),
    )(grad_out, gate_pre, up_pre, weight, block_mask)


def solution(mesh):
    placed = (P("col", "row"), P("col", "row"), P("row", "col"), P("row", "col"), P("row", "col"))
    return jax.shard_map(
        shards,
        mesh=mesh,
        in_specs=placed,
        out_specs=(P("row", "col"), P("col", "row"), P("col", "row"), P("row", "col")),
        check_vma=False,
    )
```

```python
import jax
import jax.numpy as jnp
from jax import lax
from jax.experimental import pallas as pl
from jax.experimental.pallas import tpu as pltpu
from jax.sharding import PartitionSpec as P

NZ, NX, NY = 8, 4, 4
SHARD = 128
CUT = 32
REST = SHARD - CUT
MESH = pl.DeviceIdType.MESH
F32 = jnp.float32
BF16 = jnp.bfloat16
ORDER = (4, 3, -3, 2, -2, 1, -1, 0)


class Slots:
    def __init__(self):
        self.known = {}

    def __call__(self, *key):
        return self.known.setdefault(key, len(self.known))


def dot(a, b, a_dim, b_dim):
    return lax.dot_general(a, b, (((a_dim,), (b_dim,)), ((), ())), preferred_element_type=F32)


def tile(n, size):
    return pl.ds(pl.multiple_of(n * size, size), size)


def kernel(
    grad_ref, gate_ref, up_ref, weight_ref, mask_ref,
    out_ref, dgate_ref, dup_ref, dweight_ref,
    gall, hall, hx, part, wm, wo, dpart, acc, accx, wsend, wrecv,
    land_a, land_b, land_s, land_y, land_x,
    send_sem, recv_sem,
):
    row, col = lax.axis_index("row"), lax.axis_index("col")
    z, x = row // NX, row % NX
    y, core = col // 2, col % 2
    parity = x % 2
    near = 1 - 2 * parity

    def zi(o):
        return lax.rem(z + (o + NZ), NZ)

    def xi(d):
        return lax.rem(x + (d + NX), NX)

    def yi(d):
        return lax.rem(y + (d + NY), NY)

    def zdev(d):
        return (zi(d) * NX + x, col)

    def xdev(d):
        return (z * NX + xi(d), col)

    def ydev(d):
        return (row, yi(d) * 2 + core)

    sibling = (row, y * 2 + (1 - core))
    mates = (xdev(near), xdev(-near))
    across = xdev(2)

    sems, slot_a, slot_b = Slots(), Slots(), Slots()
    sends = []

    def send(src, dst, dev, *key):
        copy = pltpu.make_async_remote_copy(
            src_ref=src, dst_ref=dst, send_sem=send_sem.at[len(sends)],
            recv_sem=recv_sem.at[sems(*key)], device_id=dev, device_id_type=MESH,
        )
        copy.start()
        sends.append(copy)

    def arrive(dst, *key):
        pltpu.make_async_remote_copy(
            src_ref=dst, dst_ref=dst, send_sem=send_sem.at[0],
            recv_sem=recv_sem.at[sems(*key)], device_id=sibling, device_id_type=MESH,
        ).wait_recv()

    def add(dst, rows, *terms):
        @pl.loop(0, rows // 16)
        def _(i):
            at = tile(i, 16)
            total = terms[0].at[at, :][...].astype(F32)
            for term in terms[1:]:
                total = total + term.at[at, :][...].astype(F32)
            dst.at[at, :][...] = total.astype(BF16)

    barrier = pltpu.get_barrier_semaphore()
    for dev in (zdev(1), zdev(-1), xdev(1), xdev(-1), across, ydev(1), ydev(-1), sibling):
        pl.semaphore_signal(barrier, inc=1, device_id=dev, device_id_type=MESH)

    mine, other = x // 2, 1 - x // 2

    @pl.loop(0, SHARD // 16)
    def _(i):
        gall[z, pl.ds(pl.multiple_of(mine * SHARD + i * 16, 16), 16), :] = grad_ref[tile(i, 16), :]

    def hidden_into(dst, which):
        for j in (0, 1):
            @pl.loop(0, 4)
            def _(i):
                at = pl.ds(pl.multiple_of((which + 2 * j) * SHARD + i * 32, 32), 32)
                g = gate_ref[at, :].astype(F32)
                u = up_ref[at, :].astype(F32)
                dst.at[pl.ds(pl.multiple_of(j * SHARD + i * 32, 32), 32), :][...] = (
                    g * jax.nn.sigmoid(g) * u
                ).astype(BF16)

    hidden_into(hx, 1 - parity)
    hidden_into(hall.at[0, col], parity)

    pl.semaphore_wait(barrier, 8)

    def rows_a(buf, o, e):
        return buf.at[zi(o), pl.ds(pl.multiple_of((other if e else mine) * SHARD, 16), CUT), :]

    def rows_b(buf, o, e):
        return buf.at[zi(o), pl.ds(pl.multiple_of((other if e else mine) * SHARD + CUT, 16), REST), :]

    def ga(o, e):
        return rows_a(gall, o, e)

    def gb(o, e):
        return rows_b(gall, o, e)

    def hid(f, dy, h=None):
        at = slice(None) if h is None else pl.ds(h * 128, 128)
        return hall.at[f, yi(dy) * 2 + core, at, :]

    def hid_sibling(f, dy):
        return hall.at[f, yi(dy) * 2 + (1 - core)]

    def az_next(o):
        if o <= 0 and o > -4:
            send(ga(o, 0), ga(o, 0), zdev(1), "gaz", o - 1)
        if o >= 0 and o < 3:
            send(ga(o, 0), ga(o, 0), zdev(-1), "gaz", o + 1)

    def ax_send(o):
        send(ga(o, 0), ga(o, 0), across, "gax", o)

    def az(*offsets):
        for o in offsets:
            arrive(ga(o, 0), "gaz", o)
            az_next(o)
            ax_send(o)

    def ax(*offsets):
        for o in offsets:
            arrive(ga(o, 1), "gax", o)

    def bz_first(e):
        send(gb(0, e), gb(0, e), zdev(1), "gbz", e, -1)
        send(gb(0, e), gb(0, e), zdev(-1), "gbz", e, 1)

    def bx():
        arrive(gb(0, 1), "gbx")
        bz_first(1)

    def bz(k, e):
        low, high = (-4, 3) if e == 0 else (-3, 4)
        for o in (-k, k):
            if o < low or o > high:
                continue
            arrive(gb(o, e), "gbz", e, o)
            if o < 0 and o > low:
                send(gb(o, e), gb(o, e), zdev(1), "gbz", e, o - 1)
            if o > 0 and o < high:
                send(gb(o, e), gb(o, e), zdev(-1), "gbz", e, o + 1)

    def h0(f):
        for h in (0, 1):
            send(hid(f, 0, h), hid(f, 0, h), ydev(1), "hy", f, -1, h)
            send(hid(f, 0, 1 - h), hid(f, 0, 1 - h), ydev(-1), "hy", f, 1, 1 - h)
        send(hid(f, 0), hid(f, 0), sibling, "hs", f, 0)

    def h1(f):
        arrive(hid(f, -1, 0), "hy", f, -1, 0)
        send(hid(f, -1, 0), hid(f, -1, 0), ydev(1), "hy2", f, 0)
        arrive(hid(f, 1, 1), "hy", f, 1, 1)
        send(hid(f, 1, 1), hid(f, 1, 1), ydev(-1), "hy2", f, 1)

    def h2(f):
        arrive(hid(f, -1, 1), "hy", f, -1, 1)
        send(hid(f, -1), hid(f, -1), sibling, "hs", f, -1)
        arrive(hid(f, 1, 0), "hy", f, 1, 0)
        send(hid(f, 1), hid(f, 1), sibling, "hs", f, 1)

    def h3(f):
        arrive(hid(f, 2, 0), "hy2", f, 0)
        arrive(hid(f, 2, 1), "hy2", f, 1)
        send(hid(f, 2), hid(f, 2), sibling, "hs", f, 2)

    def h4(f):
        for dy in (0, -1, 1, 2):
            arrive(hid_sibling(f, dy), "hs", f, dy)

    def mm_part(o):
        block = zi(o)
        for s in (0, 1):
            @pl.loop(0, 2)
            def _(n):
                at = tile(n, 256)
                part[block, :, pl.ds(pl.multiple_of(s * 512 + n * 256, 256), 256)] = (
                    dot(hall[0, block], wm[s, :, at], 1, 0) + dot(hall[1 + s, block], wo[s, :, at], 1, 0)
                ).astype(BF16)

    def mm_dpart(block):
        @pl.loop(0, 2)
        def _(n):
            at = tile(n, 256)
            first, second = gall[block, :, pl.ds(0, 512)], gall[block, :, pl.ds(512, 512)]
            dpart[1, block, :, at] = dot(first, wo[0, at, :], 1, 1).astype(BF16)
            dpart[2, block, :, at] = dot(second, wo[1, at, :], 1, 1).astype(BF16)
            dpart[0, block, :, at] = (dot(first, wm[0, at, :], 1, 1) + dot(second, wm[1, at, :], 1, 1)).astype(BF16)

    def mm_weight(k):
        pair = pl.ds(2 * k, 2)

        def gsum(dst, at, f, cols):
            product = dot(
                hall[f, pair].reshape(512, 512), gall[pair, :, cols].reshape(512, 256), 0, 0
            )
            dst[:, at] = product if k == 0 else dst[:, at] + product

        for s in (0, 1):
            @pl.loop(0, 2)
            def _(n):
                gsum(accx.at[s], tile(n, 256), 1 + s, pl.ds(pl.multiple_of(s * 512 + n * 256, 256), 256))

        @pl.loop(0, 4)
        def _(n):
            gsum(acc, tile(n, 256), 0, tile(n, 256))

    def pa(o, e):
        return rows_a(part, o, e)

    def pb(o, e):
        return rows_b(part, o, e)

    def la(*key):
        return land_a.at[slot_a(*key)]

    def lb(*key):
        return land_b.at[slot_b(*key)]

    def xs(o):
        send(pa(o, 1), la("px", o), across, "px", o)

    def zf(o):
        sides = []
        if 0 <= o < 4:
            sides.append(-1)
        if -3 < o <= 0:
            sides.append(1)
        held = la("px", o)
        arrive(held, "px", o)
        terms = [pa(o, 0), held]
        for side in sides:
            arrive(la("pz", o, side), "pz", o, side)
            terms.append(la("pz", o, side))
        if o == 0:
            add(out_ref.at[pl.ds(0, CUT), :], CUT, *terms)
            return
        add(held, CUT, *terms)
        if o > 0:
            send(held, la("pz", o - 1, -1), zdev(1), "pz", o - 1, -1)
        else:
            send(held, la("pz", o + 1, 1), zdev(-1), "pz", o + 1, 1)

    def rz(o):
        for e in (1, 0):
            sides = []
            if 0 <= o < 4 and not (o == 3 and e == 1):
                sides.append(-1)
            if -4 < o <= 0 and not (o == -3 and e == 0):
                sides.append(1)
            terms = [pb(o, e)]
            for side in sides:
                held = lb("pbz", e, o, side)
                arrive(held, "pbz", e, o, side)
                terms.append(held)
            src = terms[-1]
            if len(terms) > 1:
                add(src, REST, *terms)
            if o == 4:
                if e == 0:
                    send(src, lb("pbz", e, 3, -1), zdev(1), "pbz", e, 3, -1)
                else:
                    send(src, lb("pbz", e, -3, 1), zdev(-1), "pbz", e, -3, 1)
            elif o > 0:
                send(src, lb("pbz", e, o - 1, -1), zdev(1), "pbz", e, o - 1, -1)
            elif o < 0:
                send(src, lb("pbz", e, o + 1, 1), zdev(-1), "pbz", e, o + 1, 1)
            elif e == 1:
                send(src, lb("pbx"), across, "pbx")

    def bf():
        held = lb("pbx")
        arrive(held, "pbx")
        add(out_ref.at[pl.ds(CUT, REST), :], REST, lb("pbz", 0, 0, 1), held)

    S = {2: 0, -1: 1, 1: 2, 0: 3}
    Y = {("m", -1): 0, ("m", 1): 1, (-1, 0): 2, (-1, 1): 3, (1, 0): 4, (1, 1): 5}
    FS = (1, 2, 0)

    def own(dy):
        return yi(dy) * 2 + core

    def dhalf(f, dy, h):
        return dpart.at[f, own(dy), pl.ds(h * 128, 128), :]

    def ly(f, *key):
        return land_y.at[f, Y[key]]

    def dsib(dy):
        block = yi(dy) * 2 + (1 - core)
        mm_dpart(block)
        for f in FS:
            send(dpart.at[f, block], land_s.at[f, S[dy]], sibling, "ds", f, dy)
        mm_dpart(own(dy))

    def dadd(dy):
        for f in FS:
            held = land_s.at[f, S[dy]]
            arrive(held, "ds", f, dy)
            here = dpart.at[f, own(dy)]
            add(here, 256, here, held)
            if dy == 2:
                send(dhalf(f, 2, 0), ly(f, "m", -1), ydev(1), "dym", f, -1)
                send(dhalf(f, 2, 1), ly(f, "m", 1), ydev(-1), "dym", f, 1)
            if dy == 1:
                send(dhalf(f, 1, 1), ly(f, -1, 1), ydev(1), "dyf", f, -1, 1)
            if dy == -1:
                send(dhalf(f, -1, 0), ly(f, 1, 0), ydev(-1), "dyf", f, 1, 0)

    def dmid(f):
        for side, h in ((-1, 0), (1, 1)):
            held = ly(f, "m", side)
            arrive(held, "dym", f, side)
            add(held, 128, held, dhalf(f, -side, h))
            send(held, ly(f, side, h), ydev(-side), "dyf", f, side, h)

    def dend(f):
        for h in (1, 0):
            for side in (-1, 1):
                arrive(ly(f, side, h), "dyf", f, side, h)

    def dmate(f):
        dend(f)
        for h in (0, 1):
            add(dhalf(f, 0, h), 128, dhalf(f, 0, h), ly(f, -1, h), ly(f, 1, h))
        send(dpart.at[f, own(0)], land_x.at[f - 1], mates[f - 1], "dx", f)

    def grads(which, j, *terms):
        @pl.loop(0, 4)
        def _(i):
            at = tile(i, 32)
            rows = pl.ds(pl.multiple_of((which + 2 * j) * SHARD + i * 32, 32), 32)
            dh = terms[0].at[at, :][...].astype(F32)
            for term in terms[1:]:
                dh = dh + term.at[at, :][...].astype(F32)
            g = gate_ref[rows, :].astype(F32)
            u = up_ref[rows, :].astype(F32)
            sig = jax.nn.sigmoid(g)
            dup_ref[rows, :] = (dh * g * sig).astype(BF16)
            dgate_ref[rows, :] = (dh * u * sig * (1.0 + g * (1.0 - sig))).astype(BF16)

    def grads_own():
        dend(0)
        for h in (0, 1):
            grads(parity, h, dhalf(0, 0, h), ly(0, -1, h), ly(0, 1, h))

    def grads_mates():
        for f in (1, 2):
            arrive(land_x.at[f - 1], "dx", f)
        for h in (0, 1):
            at = pl.ds(h * 128, 128)
            grads(1 - parity, h, land_x.at[0, at, :], land_x.at[1, at, :])

    def keep(i, j):
        return mask_ref[i, j].astype(F32)

    def mask_weights():
        @pl.loop(0, 4)
        def _(i):
            for j in range(8):
                wm[j // 4, tile(i, 128), pl.ds(j % 4 * 128, 128)] = (
                    weight_ref[tile(i, 128), pl.ds(j * 128, 128)].astype(F32) * keep(i, j)
                ).astype(BF16)

    def weights_out():
        for s in (0, 1):
            send(wm.at[s], wo.at[s], mates[s], "w", s)

    def weights_in():
        for s in (0, 1):
            arrive(wo.at[s], "w", s)

    def dweights_out():
        for s in (0, 1):
            @pl.loop(0, 16)
            def _(i):
                wsend[s, tile(i, 32), :] = accx[s, tile(i, 32), :].astype(BF16)
            send(wsend.at[s], wrecv.at[s], mates[s], "dw", s)

    def dweights_in():
        for s in (0, 1):
            arrive(wrecv.at[s], "dw", s)

        @pl.loop(0, 4)
        def _(i):
            for j in range(8):
                cols = pl.ds(j * 128, 128)
                total = acc[tile(i, 128), cols] + wrecv[j // 4, tile(i, 128), pl.ds(j % 4 * 128, 128)].astype(F32)
                dweight_ref[tile(i, 128), cols] = (total * keep(i, j)).astype(BF16)

    bz_first(0)
    az_next(0)
    for s in (0, 1):
        send(hx, hall.at[1 + s, col], mates[s], "hx", s)
    send(gb(0, 0), gb(0, 0), across, "gbx")
    h0(0)
    ax_send(0)
    mask_weights()
    h1(0)
    bz(1, 0)
    for s in (0, 1):
        arrive(hall.at[1 + s, col], "hx", s)
    h0(1)
    h0(2)
    az(-1, 1)
    h2(0)
    h3(0)
    bx()
    weights_out()
    bz(2, 0)
    h1(1)
    bz(1, 1)
    h2(1)
    az(-2, 2)
    h3(1)
    bz(3, 0)
    h1(2)
    h2(2)
    bz(2, 1)
    az(-3, 3)
    h3(2)
    weights_in()
    for f in (0, 1, 2):
        h4(f)
    mm_part(ORDER[0])
    bz(4, 0)
    mm_part(ORDER[1])
    bz(3, 1)
    mm_part(ORDER[2])
    xs(ORDER[0])
    rz(ORDER[0])
    az(-4)
    bz(4, 1)
    mm_part(ORDER[3])
    xs(ORDER[1])
    ax(0, -1, 1, -2, 2, -3, 3, -4)

    def tick(t):
        if 1 <= t < 7:
            xs(ORDER[t + 1])
        if 1 <= t <= 7:
            rz(ORDER[t])
        if 1 <= t <= 8:
            zf(ORDER[t - 1])
        if t + 3 < 8 and t >= 1:
            mm_part(ORDER[t + 3])

    dsib(2)
    tick(1)
    dsib(-1)
    dadd(2)
    tick(2)
    dsib(1)
    dadd(-1)
    tick(3)
    dadd(1)
    dmid(1)
    dsib(0)
    tick(4)
    dmid(2)
    dadd(0)
    dmid(0)
    mm_weight(0)
    mm_weight(1)
    tick(5)
    mm_weight(2)
    mm_weight(3)
    dweights_out()
    dmate(1)
    tick(6)
    dmate(2)
    tick(7)
    grads_own()
    dweights_in()
    grads_mates()
    tick(8)
    bf()

    for copy in sends:
        copy.wait_send()


def shards(gate_pre, up_pre, weight, block_mask, grad_out):
    vmem = pl.BlockSpec(memory_space=pltpu.VMEM)
    return pl.pallas_call(
        kernel,
        out_shape=(
            jax.ShapeDtypeStruct((SHARD, 1024), BF16),
            jax.ShapeDtypeStruct((512, 512), BF16),
            jax.ShapeDtypeStruct((512, 512), BF16),
            jax.ShapeDtypeStruct((512, 1024), BF16),
        ),
        in_specs=[vmem] * 4 + [pl.BlockSpec(memory_space=pltpu.SMEM)],
        out_specs=[vmem] * 4,
        scratch_shapes=[
            pltpu.VMEM((NZ, 256, 1024), BF16),
            pltpu.VMEM((3, 8, 256, 512), BF16),
            pltpu.VMEM((256, 512), BF16),
            pltpu.VMEM((NZ, 256, 1024), BF16),
            pltpu.VMEM((2, 512, 512), BF16),
            pltpu.VMEM((2, 512, 512), BF16),
            pltpu.VMEM((3, 8, 256, 512), BF16),
            pltpu.VMEM((512, 1024), F32),
            pltpu.VMEM((2, 512, 512), F32),
            pltpu.VMEM((2, 512, 512), BF16),
            pltpu.VMEM((2, 512, 512), BF16),
            pltpu.VMEM((15, CUT, 1024), BF16),
            pltpu.VMEM((15, REST, 1024), BF16),
            pltpu.VMEM((3, 4, 256, 512), BF16),
            pltpu.VMEM((3, 6, 128, 512), BF16),
            pltpu.VMEM((2, 256, 512), BF16),
            pltpu.SemaphoreType.DMA((128,)),
            pltpu.SemaphoreType.DMA((128,)),
        ],
        compiler_params=pltpu.CompilerParams(
            collective_id=0, has_side_effects=True, vmem_limit_bytes=58 * 2**20
        ),
        cost_estimate=pl.CostEstimate(flops=12 * 2**30, bytes_accessed=8 * 2**20, transcendentals=2**19),
    )(grad_out, gate_pre, up_pre, weight, block_mask)


def solution(mesh):
    placed = (P("col", "row"), P("col", "row"), P("row", "col"), P("row", "col"), P("row", "col"))
    return jax.shard_map(
        shards,
        mesh=mesh,
        in_specs=placed,
        out_specs=(P("row", "col"), P("col", "row"), P("col", "row"), P("row", "col")),
        check_vma=False,
    )
```

```python
import jax
import jax.numpy as jnp
from jax import lax
from jax.experimental import pallas as pl
from jax.experimental.pallas import tpu as pltpu
from jax.sharding import PartitionSpec as P

NZ, NX, NY = 8, 4, 4
SHARD = 128
CUT = 48
REST = SHARD - CUT
MESH = pl.DeviceIdType.MESH
F32 = jnp.float32
BF16 = jnp.bfloat16


class Slots:
    def __init__(self):
        self.known = {}

    def __call__(self, *key):
        return self.known.setdefault(key, len(self.known))


def dot(a, b, a_dim, b_dim):
    return lax.dot_general(a, b, (((a_dim,), (b_dim,)), ((), ())), preferred_element_type=F32)


def tile(n, size):
    return pl.ds(pl.multiple_of(n * size, size), size)


def kernel(
    grad_ref, gate_ref, up_ref, weight_ref, mask_ref,
    out_ref, dgate_ref, dup_ref, dweight_ref,
    gall, hall, hx, part, wm, wo, dpart, acc, accx, wsend, wrecv,
    land_a, land_b, land_s, land_y, land_x,
    send_sem, recv_sem,
):
    row, col = lax.axis_index("row"), lax.axis_index("col")
    z, x = row // NX, row % NX
    y, core = col // 2, col % 2
    parity = x % 2
    near = 1 - 2 * parity

    def zi(o):
        return lax.rem(z + (o + NZ), NZ)

    def xi(d):
        return lax.rem(x + (d + NX), NX)

    def yi(d):
        return lax.rem(y + (d + NY), NY)

    def zdev(d):
        return (zi(d) * NX + x, col)

    def xdev(d):
        return (z * NX + xi(d), col)

    def ydev(d):
        return (row, yi(d) * 2 + core)

    sibling = (row, y * 2 + (1 - core))
    mates = (xdev(near), xdev(-near))
    across = xdev(2)

    sems, slot_a, slot_b = Slots(), Slots(), Slots()
    sends = []

    def send(src, dst, dev, *key):
        copy = pltpu.make_async_remote_copy(
            src_ref=src, dst_ref=dst, send_sem=send_sem.at[len(sends)],
            recv_sem=recv_sem.at[sems(*key)], device_id=dev, device_id_type=MESH,
        )
        copy.start()
        sends.append(copy)

    def arrive(dst, *key):
        pltpu.make_async_remote_copy(
            src_ref=dst, dst_ref=dst, send_sem=send_sem.at[0],
            recv_sem=recv_sem.at[sems(*key)], device_id=sibling, device_id_type=MESH,
        ).wait_recv()

    def add(dst, rows, *terms):
        @pl.loop(0, rows // 16)
        def _(i):
            at = tile(i, 16)
            total = terms[0].at[at, :][...].astype(F32)
            for term in terms[1:]:
                total = total + term.at[at, :][...].astype(F32)
            dst.at[at, :][...] = total.astype(BF16)

    barrier = pltpu.get_barrier_semaphore()
    for dev in (zdev(1), zdev(-1), xdev(1), xdev(-1), across, ydev(1), ydev(-1), sibling):
        pl.semaphore_signal(barrier, inc=1, device_id=dev, device_id_type=MESH)

    mine, other = x // 2, 1 - x // 2

    @pl.loop(0, SHARD // 16)
    def _(i):
        gall[z, pl.ds(pl.multiple_of(mine * SHARD + i * 16, 16), 16), :] = grad_ref[tile(i, 16), :]

    def hidden_into(dst, which):
        for j in (0, 1):
            @pl.loop(0, 4)
            def _(i):
                at = pl.ds(pl.multiple_of((which + 2 * j) * SHARD + i * 32, 32), 32)
                g = gate_ref[at, :].astype(F32)
                u = up_ref[at, :].astype(F32)
                dst.at[pl.ds(pl.multiple_of(j * SHARD + i * 32, 32), 32), :][...] = (
                    g * jax.nn.sigmoid(g) * u
                ).astype(BF16)

    hidden_into(hx, 1 - parity)
    hidden_into(hall.at[0, col], parity)

    pl.semaphore_wait(barrier, 8)

    def rows_a(buf, o, e):
        return buf.at[zi(o), pl.ds(pl.multiple_of((other if e else mine) * SHARD, 16), CUT), :]

    def rows_b(buf, o, e):
        return buf.at[zi(o), pl.ds(pl.multiple_of((other if e else mine) * SHARD + CUT, 16), REST), :]

    def ga(o, e):
        return rows_a(gall, o, e)

    def gb(o, e):
        return rows_b(gall, o, e)

    def hid(f, dy, h=None):
        at = slice(None) if h is None else pl.ds(h * 128, 128)
        return hall.at[f, yi(dy) * 2 + core, at, :]

    def hid_sibling(f, dy):
        return hall.at[f, yi(dy) * 2 + (1 - core)]

    def az_next(o):
        if o <= 0 and o > -4:
            send(ga(o, 0), ga(o, 0), zdev(1), "gaz", o - 1)
        if o >= 0 and o < 3:
            send(ga(o, 0), ga(o, 0), zdev(-1), "gaz", o + 1)

    def ax_send(o):
        send(ga(o, 0), ga(o, 0), across, "gax", o)

    def az(*offsets):
        for o in offsets:
            arrive(ga(o, 0), "gaz", o)
            az_next(o)
            ax_send(o)

    def ax(*offsets):
        for o in offsets:
            arrive(ga(o, 1), "gax", o)

    def bz_first(e):
        send(gb(0, e), gb(0, e), zdev(1), "gbz", e, -1)
        send(gb(0, e), gb(0, e), zdev(-1), "gbz", e, 1)

    def bx():
        arrive(gb(0, 1), "gbx")
        bz_first(1)

    def bzo(o, e):
        low, high = (-4, 3) if e == 0 else (-3, 4)
        arrive(gb(o, e), "gbz", e, o)
        if o < 0 and o > low:
            send(gb(o, e), gb(o, e), zdev(1), "gbz", e, o - 1)
        if o > 0 and o < high:
            send(gb(o, e), gb(o, e), zdev(-1), "gbz", e, o + 1)

    def hx_out():
        for s in (0, 1):
            send(hx, hall.at[1 + s, col], mates[s], "hx", s)

    def hx_in():
        for s in (0, 1):
            arrive(hall.at[1 + s, col], "hx", s)

    def h0(f):
        for h in (0, 1):
            send(hid(f, 0, h), hid(f, 0, h), ydev(1), "hy", f, -1, h)
            send(hid(f, 0, 1 - h), hid(f, 0, 1 - h), ydev(-1), "hy", f, 1, 1 - h)
        send(hid(f, 0), hid(f, 0), sibling, "hs", f, 0)

    def h1(f):
        arrive(hid(f, -1, 0), "hy", f, -1, 0)
        send(hid(f, -1, 0), hid(f, -1, 0), ydev(1), "hy2", f, 0)
        arrive(hid(f, 1, 1), "hy", f, 1, 1)
        send(hid(f, 1, 1), hid(f, 1, 1), ydev(-1), "hy2", f, 1)

    def h2(f):
        arrive(hid(f, -1, 1), "hy", f, -1, 1)
        send(hid(f, -1), hid(f, -1), sibling, "hs", f, -1)
        arrive(hid(f, 1, 0), "hy", f, 1, 0)
        send(hid(f, 1), hid(f, 1), sibling, "hs", f, 1)

    def h3(f):
        arrive(hid(f, 2, 0), "hy2", f, 0)
        arrive(hid(f, 2, 1), "hy2", f, 1)
        send(hid(f, 2), hid(f, 2), sibling, "hs", f, 2)

    def h4(f):
        for dy in (0, -1, 1, 2):
            arrive(hid_sibling(f, dy), "hs", f, dy)

    def mm_part(o):
        block = zi(o)
        for s in (0, 1):
            part[block, :, pl.ds(s * 512, 512)] = (
                dot(hall[0, block], wm[s], 1, 0) + dot(hall[1 + s, block], wo[s], 1, 0)
            ).astype(BF16)

    def mm_dpart(f, block):
        first, second = gall[block, :, pl.ds(0, 512)], gall[block, :, pl.ds(512, 512)]
        if f == 0:
            product = dot(first, wm[0], 1, 1) + dot(second, wm[1], 1, 1)
        else:
            product = dot((first, second)[f - 1], wo[f - 1], 1, 1)
        dpart[f, block] = product.astype(BF16)

    def mm_sum(dst, f, s):
        for k in (0, 1):
            blocks = pl.ds(4 * k, 4)
            product = dot(
                hall[f, blocks].reshape(1024, 512), gall[blocks, :, pl.ds(s * 512, 512)].reshape(1024, 512), 0, 0
            )
            dst[...] = product if k == 0 else dst[...] + product

    def mm_mate(s):
        mm_sum(accx.at[s], 1 + s, s)

    def mm_own(s):
        mm_sum(acc.at[s], 0, s)

    def pa(o, e):
        return rows_a(part, o, e)

    def pb(o, e):
        return rows_b(part, o, e)

    def la(*key):
        return land_a.at[slot_a(*key)]

    def lb(*key):
        return land_b.at[slot_b(*key)]

    def xs(o):
        send(pa(o, 1), la("px", o), across, "px", o)

    def zf(o):
        sides = []
        if 0 <= o < 4:
            sides.append(-1)
        if -3 < o <= 0:
            sides.append(1)
        held = la("px", o)
        arrive(held, "px", o)
        terms = [pa(o, 0), held]
        for side in sides:
            arrive(la("pz", o, side), "pz", o, side)
            terms.append(la("pz", o, side))
        if o == 0:
            add(out_ref.at[pl.ds(0, CUT), :], CUT, *terms)
            return
        add(held, CUT, *terms)
        if o > 0:
            send(held, la("pz", o - 1, -1), zdev(1), "pz", o - 1, -1)
        else:
            send(held, la("pz", o + 1, 1), zdev(-1), "pz", o + 1, 1)

    def rz(o, e):
        sides = []
        if 0 <= o < 4 and not (o == 3 and e == 1):
            sides.append(-1)
        if -4 < o <= 0 and not (o == -3 and e == 0):
            sides.append(1)
        terms = [pb(o, e)]
        for side in sides:
            held = lb("pbz", e, o, side)
            arrive(held, "pbz", e, o, side)
            terms.append(held)
        src = terms[-1]
        if len(terms) > 1:
            add(src, REST, *terms)
        if o == 4:
            if e == 0:
                send(src, lb("pbz", e, 3, -1), zdev(1), "pbz", e, 3, -1)
            else:
                send(src, lb("pbz", e, -3, 1), zdev(-1), "pbz", e, -3, 1)
        elif o > 0:
            send(src, lb("pbz", e, o - 1, -1), zdev(1), "pbz", e, o - 1, -1)
        elif o < 0:
            send(src, lb("pbz", e, o + 1, 1), zdev(-1), "pbz", e, o + 1, 1)
        elif e == 1:
            send(src, lb("pbx"), across, "pbx")

    def bf():
        held = lb("pbx")
        arrive(held, "pbx")
        add(out_ref.at[pl.ds(CUT, REST), :], REST, lb("pbz", 0, 0, 1), held)

    S = {2: 0, -1: 1, 1: 2, 0: 3}
    Y = {("m", -1): 0, ("m", 1): 1, (-1, 0): 2, (-1, 1): 3, (1, 0): 4, (1, 1): 5}
    DYS = (2, -1, 1, 0)

    def own(dy):
        return yi(dy) * 2 + core

    def dhalf(f, dy, h):
        return dpart.at[f, own(dy), pl.ds(h * 128, 128), :]

    def ly(f, *key):
        return land_y.at[f, Y[key]]

    def dsib(f):
        for dy in DYS:
            block = yi(dy) * 2 + (1 - core)
            mm_dpart(f, block)
            send(dpart.at[f, block], land_s.at[f, S[dy]], sibling, "ds", f, dy)

    def down(f):
        for dy in DYS:
            mm_dpart(f, own(dy))

    def dadd(f):
        for dy in DYS:
            held = land_s.at[f, S[dy]]
            arrive(held, "ds", f, dy)
            here = dpart.at[f, own(dy)]
            add(here, 256, here, held)
            if dy == 2:
                send(dhalf(f, 2, 0), ly(f, "m", -1), ydev(1), "dym", f, -1)
                send(dhalf(f, 2, 1), ly(f, "m", 1), ydev(-1), "dym", f, 1)
            if dy == 1:
                send(dhalf(f, 1, 1), ly(f, -1, 1), ydev(1), "dyf", f, -1, 1)
            if dy == -1:
                send(dhalf(f, -1, 0), ly(f, 1, 0), ydev(-1), "dyf", f, 1, 0)

    def dmid(f):
        for side, h in ((-1, 0), (1, 1)):
            held = ly(f, "m", side)
            arrive(held, "dym", f, side)
            add(held, 128, held, dhalf(f, -side, h))
            send(held, ly(f, side, h), ydev(-side), "dyf", f, side, h)

    def dend(f):
        for h in (1, 0):
            for side in (-1, 1):
                arrive(ly(f, side, h), "dyf", f, side, h)

    def dmate(f):
        dend(f)
        for h in (0, 1):
            add(dhalf(f, 0, h), 128, dhalf(f, 0, h), ly(f, -1, h), ly(f, 1, h))
        send(dpart.at[f, own(0)], land_x.at[f - 1], mates[f - 1], "dx", f)

    def grads(which, j, *terms):
        @pl.loop(0, 4)
        def _(i):
            at = tile(i, 32)
            rows = pl.ds(pl.multiple_of((which + 2 * j) * SHARD + i * 32, 32), 32)
            dh = terms[0].at[at, :][...].astype(F32)
            for term in terms[1:]:
                dh = dh + term.at[at, :][...].astype(F32)
            g = gate_ref[rows, :].astype(F32)
            u = up_ref[rows, :].astype(F32)
            sig = jax.nn.sigmoid(g)
            dup_ref[rows, :] = (dh * g * sig).astype(BF16)
            dgate_ref[rows, :] = (dh * u * sig * (1.0 + g * (1.0 - sig))).astype(BF16)

    def grads_own():
        dend(0)
        for h in (0, 1):
            grads(parity, h, dhalf(0, 0, h), ly(0, -1, h), ly(0, 1, h))

    def grads_mates():
        for f in (1, 2):
            arrive(land_x.at[f - 1], "dx", f)
        for h in (0, 1):
            at = pl.ds(h * 128, 128)
            grads(1 - parity, h, land_x.at[0, at, :], land_x.at[1, at, :])

    def keep(i, j):
        return mask_ref[i, j].astype(F32)

    def mask_weights():
        @pl.loop(0, 4)
        def _(i):
            for j in range(8):
                wm[j // 4, tile(i, 128), pl.ds(j % 4 * 128, 128)] = (
                    weight_ref[tile(i, 128), pl.ds(j * 128, 128)].astype(F32) * keep(i, j)
                ).astype(BF16)

    def weights_out():
        for s in (0, 1):
            send(wm.at[s], wo.at[s], mates[s], "w", s)

    def weights_in():
        for s in (0, 1):
            arrive(wo.at[s], "w", s)

    def dweights_out():
        for s in (0, 1):
            @pl.loop(0, 16)
            def _(i):
                wsend[s, tile(i, 32), :] = accx[s, tile(i, 32), :].astype(BF16)
            send(wsend.at[s], wrecv.at[s], mates[s], "dw", s)

    def dweights_in():
        for s in (0, 1):
            arrive(wrecv.at[s], "dw", s)

        @pl.loop(0, 4)
        def _(i):
            for j in range(8):
                at = (j // 4, tile(i, 128), pl.ds(j % 4 * 128, 128))
                dweight_ref[tile(i, 128), pl.ds(j * 128, 128)] = (
                    (acc[at] + wrecv[at].astype(F32)) * keep(i, j)
                ).astype(BF16)

    send(gb(0, 0), gb(0, 0), across, "gbx")
    hx_out()
    az_next(0)
    ax_send(0)
    mask_weights()
    bz_first(0)
    h0(0)
    az(1)
    az(-1)
    bx()
    weights_out()
    h1(0)
    bzo(1, 0)
    bzo(-1, 0)
    h2(0)
    az(-2)
    az(2)
    hx_in()
    h0(2)
    h0(1)
    h3(0)
    ax(0)
    bzo(1, 1)
    bzo(-1, 1)
    h4(0)
    ax(1)
    h1(2)
    bzo(2, 0)
    bzo(-2, 0)
    ax(-1)
    az(-3)
    az(3)
    h2(2)
    h1(1)
    bzo(-2, 1)
    bzo(2, 1)
    h2(1)
    bzo(3, 0)
    bzo(-3, 0)
    h3(2)
    az(-4)
    weights_in()
    bzo(3, 1)
    h4(2)
    ax(-2)
    h3(1)
    bzo(-3, 1)
    ax(2)
    h4(1)
    mm_part(-1)
    mm_part(3)
    rz(3, 1)
    mm_part(4)
    xs(4)
    mm_part(-3)
    rz(-3, 0)
    mm_part(1)
    bzo(4, 1)
    xs(1)
    xs(-3)
    ax(-3)
    mm_part(2)
    xs(2)
    ax(3)
    xs(3)
    mm_part(-2)
    rz(4, 1)
    mm_part(0)
    xs(0)
    rz(4, 0)
    xs(-2)
    bzo(-4, 0)
    xs(-1)
    ax(-4)
    dsib(2)
    mm_mate(1)
    zf(4)
    down(2)
    dsib(1)
    dadd(2)
    down(1)
    rz(-3, 1)
    zf(-3)
    rz(2, 1)
    rz(3, 0)
    dadd(1)
    dsib(0)
    down(0)
    mm_mate(0)
    dweights_out()
    rz(-2, 1)
    zf(3)
    dmid(2)
    rz(1, 1)
    mm_own(0)
    zf(-2)
    rz(-2, 0)
    dmid(1)
    rz(2, 0)
    dadd(0)
    mm_own(1)
    rz(-1, 1)
    zf(2)
    zf(-1)
    dmate(2)
    dmate(1)
    rz(-1, 0)
    rz(1, 0)
    dmid(0)
    dweights_in()
    rz(0, 1)
    zf(1)
    grads_own()
    grads_mates()
    zf(0)
    rz(0, 0)
    bf()

    for copy in sends:
        copy.wait_send()


def shards(gate_pre, up_pre, weight, block_mask, grad_out):
    vmem = pl.BlockSpec(memory_space=pltpu.VMEM)
    return pl.pallas_call(
        kernel,
        out_shape=(
            jax.ShapeDtypeStruct((SHARD, 1024), BF16),
            jax.ShapeDtypeStruct((512, 512), BF16),
            jax.ShapeDtypeStruct((512, 512), BF16),
            jax.ShapeDtypeStruct((512, 1024), BF16),
        ),
        in_specs=[vmem] * 4 + [pl.BlockSpec(memory_space=pltpu.SMEM)],
        out_specs=[vmem] * 4,
        scratch_shapes=[
            pltpu.VMEM((NZ, 256, 1024), BF16),
            pltpu.VMEM((3, 8, 256, 512), BF16),
            pltpu.VMEM((256, 512), BF16),
            pltpu.VMEM((NZ, 256, 1024), BF16),
            pltpu.VMEM((2, 512, 512), BF16),
            pltpu.VMEM((2, 512, 512), BF16),
            pltpu.VMEM((3, 8, 256, 512), BF16),
            pltpu.VMEM((2, 512, 512), F32),
            pltpu.VMEM((2, 512, 512), F32),
            pltpu.VMEM((2, 512, 512), BF16),
            pltpu.VMEM((2, 512, 512), BF16),
            pltpu.VMEM((15, CUT, 1024), BF16),
            pltpu.VMEM((15, REST, 1024), BF16),
            pltpu.VMEM((3, 4, 256, 512), BF16),
            pltpu.VMEM((3, 6, 128, 512), BF16),
            pltpu.VMEM((2, 256, 512), BF16),
            pltpu.SemaphoreType.DMA((128,)),
            pltpu.SemaphoreType.DMA((128,)),
        ],
        compiler_params=pltpu.CompilerParams(
            collective_id=0, has_side_effects=True, vmem_limit_bytes=58 * 2**20
        ),
        cost_estimate=pl.CostEstimate(flops=12 * 2**30, bytes_accessed=8 * 2**20, transcendentals=2**19),
    )(grad_out, gate_pre, up_pre, weight, block_mask)


def solution(mesh):
    placed = (P("col", "row"), P("col", "row"), P("row", "col"), P("row", "col"), P("row", "col"))
    return jax.shard_map(
        shards,
        mesh=mesh,
        in_specs=placed,
        out_specs=(P("row", "col"), P("col", "row"), P("col", "row"), P("row", "col")),
        check_vma=False,
    )
```

```python
import jax
import jax.numpy as jnp
from jax import lax
from jax.experimental import pallas as pl
from jax.experimental.pallas import tpu as pltpu
from jax.sharding import PartitionSpec as P

NZ, NX, NY = 8, 4, 4
SHARD = 128
GCUT, PCUT = 32, 48
MESH = pl.DeviceIdType.MESH
F32 = jnp.float32
BF16 = jnp.bfloat16


class Slots:
    def __init__(self):
        self.known = {}

    def __call__(self, *key):
        return self.known.setdefault(key, len(self.known))


def dot(a, b, a_dim, b_dim):
    return lax.dot_general(a, b, (((a_dim,), (b_dim,)), ((), ())), preferred_element_type=F32)


def tile(n, size):
    return pl.ds(pl.multiple_of(n * size, size), size)


def kernel(
    grad_in, gate_in, up_in, weight_in, mask_ref,
    out_to, dgate_to, dup_to, dweight_to,
    gate_ref, up_ref, weight_ref, out_ref, dgate_ref, dup_ref, dweight_ref, in_sem, out_sem,
    gall, hall, hx, part, wm, wo, dpart, acc, accx, wsend, wrecv,
    land_a, land_b, land_s, land_y, land_x,
    send_sem, recv_sem,
):
    row, col = lax.axis_index("row"), lax.axis_index("col")
    z, x = row // NX, row % NX
    y, core = col // 2, col % 2
    parity = x % 2
    near = 1 - 2 * parity

    def zi(o):
        return lax.rem(z + (o + NZ), NZ)

    def xi(d):
        return lax.rem(x + (d + NX), NX)

    def yi(d):
        return lax.rem(y + (d + NY), NY)

    def zdev(d):
        return (zi(d) * NX + x, col)

    def xdev(d):
        return (z * NX + xi(d), col)

    def ydev(d):
        return (row, yi(d) * 2 + core)

    sibling = (row, y * 2 + (1 - core))
    mates = (xdev(near), xdev(-near))
    across = xdev(2)

    sems, slot_a, slot_b = Slots(), Slots(), Slots()
    sends = []

    def send(src, dst, dev, *key):
        copy = pltpu.make_async_remote_copy(
            src_ref=src, dst_ref=dst, send_sem=send_sem.at[len(sends)],
            recv_sem=recv_sem.at[sems(*key)], device_id=dev, device_id_type=MESH,
        )
        copy.start()
        sends.append(copy)

    def arrive(dst, *key):
        pltpu.make_async_remote_copy(
            src_ref=dst, dst_ref=dst, send_sem=send_sem.at[0],
            recv_sem=recv_sem.at[sems(*key)], device_id=sibling, device_id_type=MESH,
        ).wait_recv()

    def add(dst, rows, *terms):
        @pl.loop(0, rows // 16)
        def _(i):
            at = tile(i, 16)
            total = terms[0].at[at, :][...].astype(F32)
            for term in terms[1:]:
                total = total + term.at[at, :][...].astype(F32)
            dst.at[at, :][...] = total.astype(BF16)

    barrier = pltpu.get_barrier_semaphore()
    for dev in (zdev(1), zdev(-1), xdev(1), xdev(-1), across, ydev(1), ydev(-1), sibling):
        pl.semaphore_signal(barrier, inc=1, device_id=dev, device_id_type=MESH)

    mine, other = x // 2, 1 - x // 2
    taken = {}
    for n, (name, src, dst) in enumerate((
        ("grad", grad_in, gall.at[z, pl.ds(pl.multiple_of(mine * SHARD, SHARD), SHARD), :]),
        ("gate", gate_in, gate_ref),
        ("up", up_in, up_ref),
        ("weight", weight_in, weight_ref),
    )):
        taken[name] = pltpu.make_async_copy(src, dst, in_sem.at[n])
        taken[name].start()
    results = ((out_ref, out_to), (dgate_ref, dgate_to), (dup_ref, dup_to), (dweight_ref, dweight_to))
    given = [pltpu.make_async_copy(src, dst, out_sem.at[n]) for n, (src, dst) in enumerate(results)]

    def hidden_into(dst, which):
        for j in (0, 1):
            @pl.loop(0, 4)
            def _(i):
                at = pl.ds(pl.multiple_of((which + 2 * j) * SHARD + i * 32, 32), 32)
                g = gate_ref[at, :].astype(F32)
                u = up_ref[at, :].astype(F32)
                dst.at[pl.ds(pl.multiple_of(j * SHARD + i * 32, 32), 32), :][...] = (
                    g * jax.nn.sigmoid(g) * u
                ).astype(BF16)

    pl.semaphore_wait(barrier, 8)
    taken["grad"].wait()

    def rows(buf, o, e, start, size):
        return buf.at[zi(o), pl.ds(pl.multiple_of((other if e else mine) * SHARD + start, 16), size), :]

    def ga(o, e):
        return rows(gall, o, e, 0, GCUT)

    def gb(o, e):
        return rows(gall, o, e, GCUT, SHARD - GCUT)

    def hid(f, dy, h=None):
        at = slice(None) if h is None else pl.ds(h * 128, 128)
        return hall.at[f, yi(dy) * 2 + core, at, :]

    def hid_sibling(f, dy):
        return hall.at[f, yi(dy) * 2 + (1 - core)]

    def az_next(o):
        if o <= 0 and o > -4:
            send(ga(o, 0), ga(o, 0), zdev(1), "gaz", o - 1)
        if o >= 0 and o < 3:
            send(ga(o, 0), ga(o, 0), zdev(-1), "gaz", o + 1)

    def ax_send(o):
        send(ga(o, 0), ga(o, 0), across, "gax", o)

    def az(*offsets):
        for o in offsets:
            arrive(ga(o, 0), "gaz", o)
            az_next(o)
            ax_send(o)

    def ax(*offsets):
        for o in offsets:
            arrive(ga(o, 1), "gax", o)

    def bz_first(e):
        send(gb(0, e), gb(0, e), zdev(1), "gbz", e, -1)
        send(gb(0, e), gb(0, e), zdev(-1), "gbz", e, 1)

    def bx():
        arrive(gb(0, 1), "gbx")
        bz_first(1)

    def bzo(o, e):
        low, high = (-4, 3) if e == 0 else (-3, 4)
        arrive(gb(o, e), "gbz", e, o)
        if o < 0 and o > low:
            send(gb(o, e), gb(o, e), zdev(1), "gbz", e, o - 1)
        if o > 0 and o < high:
            send(gb(o, e), gb(o, e), zdev(-1), "gbz", e, o + 1)

    def hx_out():
        for s in (0, 1):
            send(hx, hall.at[1 + s, col], mates[s], "hx", s)

    def hx_in():
        for s in (0, 1):
            arrive(hall.at[1 + s, col], "hx", s)

    def h0(f):
        for h in (0, 1):
            send(hid(f, 0, h), hid(f, 0, h), ydev(1), "hy", f, -1, h)
            send(hid(f, 0, 1 - h), hid(f, 0, 1 - h), ydev(-1), "hy", f, 1, 1 - h)
        send(hid(f, 0), hid(f, 0), sibling, "hs", f, 0)

    def h1(f):
        arrive(hid(f, -1, 0), "hy", f, -1, 0)
        send(hid(f, -1, 0), hid(f, -1, 0), ydev(1), "hy2", f, 0)
        arrive(hid(f, 1, 1), "hy", f, 1, 1)
        send(hid(f, 1, 1), hid(f, 1, 1), ydev(-1), "hy2", f, 1)

    def h2(f):
        arrive(hid(f, -1, 1), "hy", f, -1, 1)
        send(hid(f, -1), hid(f, -1), sibling, "hs", f, -1)
        arrive(hid(f, 1, 0), "hy", f, 1, 0)
        send(hid(f, 1), hid(f, 1), sibling, "hs", f, 1)

    def h3(f):
        arrive(hid(f, 2, 0), "hy2", f, 0)
        arrive(hid(f, 2, 1), "hy2", f, 1)
        send(hid(f, 2), hid(f, 2), sibling, "hs", f, 2)

    def h4(f):
        for dy in (0, -1, 1, 2):
            arrive(hid_sibling(f, dy), "hs", f, dy)

    def mm_part(o):
        block = zi(o)
        for s in (0, 1):
            part[block, :, pl.ds(s * 512, 512)] = (
                dot(hall[0, block], wm[s], 1, 0) + dot(hall[1 + s, block], wo[s], 1, 0)
            ).astype(BF16)

    def mm_dpart(f, block):
        first, second = gall[block, :, pl.ds(0, 512)], gall[block, :, pl.ds(512, 512)]
        if f == 0:
            product = dot(first, wm[0], 1, 1) + dot(second, wm[1], 1, 1)
        else:
            product = dot((first, second)[f - 1], wo[f - 1], 1, 1)
        dpart[f, block] = product.astype(BF16)

    def mm_sum(dst, f, s):
        for k in (0, 1):
            blocks = pl.ds(4 * k, 4)
            product = dot(
                hall[f, blocks].reshape(1024, 512), gall[blocks, :, pl.ds(s * 512, 512)].reshape(1024, 512), 0, 0
            )
            dst[...] = product if k == 0 else dst[...] + product

    def mm_mate(s):
        mm_sum(accx.at[s], 1 + s, s)

    def mm_own(s):
        mm_sum(acc.at[s], 0, s)

    def pa(o, e):
        return rows(part, o, e, 0, PCUT)

    def pb(o, e):
        return rows(part, o, e, PCUT, SHARD - PCUT)

    def la(*key):
        return land_a.at[slot_a(*key)]

    def lb(*key):
        return land_b.at[slot_b(*key)]

    def xs(o):
        send(pa(o, 1), la("px", o), across, "px", o)

    def zf(o):
        sides = []
        if 0 <= o < 4:
            sides.append(-1)
        if -3 < o <= 0:
            sides.append(1)
        held = la("px", o)
        arrive(held, "px", o)
        terms = [pa(o, 0), held]
        for side in sides:
            arrive(la("pz", o, side), "pz", o, side)
            terms.append(la("pz", o, side))
        if o == 0:
            add(out_ref.at[pl.ds(0, PCUT), :], PCUT, *terms)
            return
        add(held, PCUT, *terms)
        if o > 0:
            send(held, la("pz", o - 1, -1), zdev(1), "pz", o - 1, -1)
        else:
            send(held, la("pz", o + 1, 1), zdev(-1), "pz", o + 1, 1)

    def rz(o, e):
        sides = []
        if 0 <= o < 4 and not (o == 3 and e == 1):
            sides.append(-1)
        if -4 < o <= 0 and not (o == -3 and e == 0):
            sides.append(1)
        terms = [pb(o, e)]
        for side in sides:
            held = lb("pbz", e, o, side)
            arrive(held, "pbz", e, o, side)
            terms.append(held)
        src = terms[-1]
        if len(terms) > 1:
            add(src, SHARD - PCUT, *terms)
        if o == 4:
            if e == 0:
                send(src, lb("pbz", e, 3, -1), zdev(1), "pbz", e, 3, -1)
            else:
                send(src, lb("pbz", e, -3, 1), zdev(-1), "pbz", e, -3, 1)
        elif o > 0:
            send(src, lb("pbz", e, o - 1, -1), zdev(1), "pbz", e, o - 1, -1)
        elif o < 0:
            send(src, lb("pbz", e, o + 1, 1), zdev(-1), "pbz", e, o + 1, 1)
        elif e == 1:
            send(src, lb("pbx"), across, "pbx")

    def bf():
        held = lb("pbx")
        arrive(held, "pbx")
        add(out_ref.at[pl.ds(PCUT, SHARD - PCUT), :], SHARD - PCUT, lb("pbz", 0, 0, 1), held)

    S = {2: 0, -1: 1, 1: 2, 0: 3}
    Y = {("m", -1): 0, ("m", 1): 1, (-1, 0): 2, (-1, 1): 3, (1, 0): 4, (1, 1): 5}
    DYS = (2, -1, 1, 0)

    def own(dy):
        return yi(dy) * 2 + core

    def dhalf(f, dy, h):
        return dpart.at[f, own(dy), pl.ds(h * 128, 128), :]

    def ly(f, *key):
        return land_y.at[f, Y[key]]

    def dsib(f):
        for dy in DYS:
            block = yi(dy) * 2 + (1 - core)
            mm_dpart(f, block)
            send(dpart.at[f, block], land_s.at[f, S[dy]], sibling, "ds", f, dy)

    def down(f):
        for dy in DYS:
            mm_dpart(f, own(dy))

    def dadd(f):
        for dy in DYS:
            held = land_s.at[f, S[dy]]
            arrive(held, "ds", f, dy)
            here = dpart.at[f, own(dy)]
            add(here, 256, here, held)
            if dy == 2:
                send(dhalf(f, 2, 0), ly(f, "m", -1), ydev(1), "dym", f, -1)
                send(dhalf(f, 2, 1), ly(f, "m", 1), ydev(-1), "dym", f, 1)
            if dy == 1:
                send(dhalf(f, 1, 1), ly(f, -1, 1), ydev(1), "dyf", f, -1, 1)
            if dy == -1:
                send(dhalf(f, -1, 0), ly(f, 1, 0), ydev(-1), "dyf", f, 1, 0)

    def dmid(f):
        for side, h in ((-1, 0), (1, 1)):
            held = ly(f, "m", side)
            arrive(held, "dym", f, side)
            add(held, 128, held, dhalf(f, -side, h))
            send(held, ly(f, side, h), ydev(-side), "dyf", f, side, h)

    def dend(f):
        for h in (1, 0):
            for side in (-1, 1):
                arrive(ly(f, side, h), "dyf", f, side, h)

    def dmate(f):
        dend(f)
        for h in (0, 1):
            add(dhalf(f, 0, h), 128, dhalf(f, 0, h), ly(f, -1, h), ly(f, 1, h))
        send(dpart.at[f, own(0)], land_x.at[f - 1], mates[f - 1], "dx", f)

    def grads(which, j, *terms):
        @pl.loop(0, 4)
        def _(i):
            at = tile(i, 32)
            rows = pl.ds(pl.multiple_of((which + 2 * j) * SHARD + i * 32, 32), 32)
            dh = terms[0].at[at, :][...].astype(F32)
            for term in terms[1:]:
                dh = dh + term.at[at, :][...].astype(F32)
            g = gate_ref[rows, :].astype(F32)
            u = up_ref[rows, :].astype(F32)
            sig = jax.nn.sigmoid(g)
            dup_ref[rows, :] = (dh * g * sig).astype(BF16)
            dgate_ref[rows, :] = (dh * u * sig * (1.0 + g * (1.0 - sig))).astype(BF16)

    def grads_own():
        dend(0)
        for h in (0, 1):
            grads(parity, h, dhalf(0, 0, h), ly(0, -1, h), ly(0, 1, h))

    def grads_mates():
        for f in (1, 2):
            arrive(land_x.at[f - 1], "dx", f)
        for h in (0, 1):
            at = pl.ds(h * 128, 128)
            grads(1 - parity, h, land_x.at[0, at, :], land_x.at[1, at, :])

    def keep(i, j):
        return mask_ref[i, j].astype(F32)

    def mask_weights():
        @pl.loop(0, 4)
        def _(i):
            for j in range(8):
                wm[j // 4, tile(i, 128), pl.ds(j % 4 * 128, 128)] = (
                    weight_ref[tile(i, 128), pl.ds(j * 128, 128)].astype(F32) * keep(i, j)
                ).astype(BF16)

    def weights_out():
        for s in (0, 1):
            send(wm.at[s], wo.at[s], mates[s], "w", s)

    def weights_in():
        for s in (0, 1):
            arrive(wo.at[s], "w", s)

    def dweights_out():
        for s in (0, 1):
            @pl.loop(0, 16)
            def _(i):
                wsend[s, tile(i, 32), :] = accx[s, tile(i, 32), :].astype(BF16)
            send(wsend.at[s], wrecv.at[s], mates[s], "dw", s)

    def dweights_in():
        for s in (0, 1):
            arrive(wrecv.at[s], "dw", s)

        @pl.loop(0, 4)
        def _(i):
            for j in range(8):
                at = (j // 4, tile(i, 128), pl.ds(j % 4 * 128, 128))
                dweight_ref[tile(i, 128), pl.ds(j * 128, 128)] = (
                    (acc[at] + wrecv[at].astype(F32)) * keep(i, j)
                ).astype(BF16)

    send(gb(0, 0), gb(0, 0), across, "gbx")
    az_next(0)
    bz_first(0)
    taken["weight"].wait()
    mask_weights()
    taken["gate"].wait()
    taken["up"].wait()
    hidden_into(hx, 1 - parity)
    hx_out()
    ax_send(0)
    hidden_into(hall.at[0, col], parity)
    h0(0)
    az(1)
    az(-1)
    bx()
    weights_out()
    h1(0)
    bzo(1, 0)
    bzo(-1, 0)
    az(2)
    az(-2)
    h2(0)
    hx_in()
    h0(1)
    h0(2)
    h3(0)
    ax(0)
    bzo(1, 1)
    bzo(-1, 1)
    ax(1)
    h4(0)
    ax(-1)
    h1(1)
    bzo(2, 0)
    bzo(-2, 0)
    az(-3)
    az(3)
    h2(1)
    h1(2)
    bzo(-2, 1)
    bzo(2, 1)
    h2(2)
    weights_in()
    bzo(-3, 0)
    bzo(3, 0)
    ax(2)
    h3(1)
    az(-4)
    ax(-2)
    h4(1)
    ax(-3)
    h3(2)
    bzo(3, 1)
    ax(3)
    bzo(-3, 1)
    h4(2)
    mm_part(4)
    rz(4, 0)
    mm_part(3)
    ax(-4)
    mm_part(0)
    xs(0)
    mm_part(1)
    rz(4, 1)
    xs(4)
    mm_part(-2)
    xs(-2)
    bzo(-4, 0)
    xs(1)
    rz(3, 1)
    mm_part(-1)
    xs(-1)
    xs(3)
    mm_part(-3)
    rz(-3, 0)
    bzo(4, 1)
    dsib(2)
    down(2)
    dsib(1)
    down(1)
    rz(-3, 1)
    zf(4)
    dadd(2)
    xs(-3)
    mm_part(2)
    rz(2, 1)
    xs(2)
    dadd(1)
    rz(-2, 0)
    rz(3, 0)
    mm_mate(1)
    mm_mate(0)
    dweights_out()
    zf(3)
    dmid(2)
    rz(1, 1)
    rz(-2, 1)
    dsib(0)
    rz(-1, 0)
    zf(-3)
    down(0)
    rz(2, 0)
    dmid(1)
    mm_own(0)
    zf(2)
    dadd(0)
    rz(-1, 1)
    mm_own(1)
    dmate(2)
    dmate(1)
    rz(1, 0)
    zf(-2)
    zf(1)
    dmid(0)
    dweights_in()
    given[3].start()
    rz(0, 1)
    zf(-1)
    rz(0, 0)
    grads_mates()
    grads_own()
    given[1].start()
    given[2].start()
    zf(0)
    bf()
    given[0].start()

    for copy in sends:
        copy.wait_send()
    for copy in given:
        copy.wait()


def hand_on(*refs):
    sources, targets, held, sem = refs[:4], refs[4:8], refs[8:12], refs[12]
    ins = [pltpu.make_async_copy(a, b, sem.at[0, n]) for n, (a, b) in enumerate(zip(sources, held))]
    outs = [pltpu.make_async_copy(a, b, sem.at[1, n]) for n, (a, b) in enumerate(zip(held, targets))]
    for copy in ins:
        copy.start()
    for first, then in zip(ins, outs):
        first.wait()
        then.start()
    for copy in outs:
        copy.wait()


def shards(gate_pre, up_pre, weight, block_mask, grad_out):
    anywhere = pl.BlockSpec(memory_space=pl.ANY)
    results = pl.pallas_call(
        kernel,
        out_shape=(
            jax.ShapeDtypeStruct((SHARD, 1024), BF16),
            jax.ShapeDtypeStruct((512, 512), BF16),
            jax.ShapeDtypeStruct((512, 512), BF16),
            jax.ShapeDtypeStruct((512, 1024), BF16),
        ),
        in_specs=[anywhere] * 4 + [pl.BlockSpec(memory_space=pltpu.SMEM)],
        out_specs=[anywhere] * 4,
        scratch_shapes=[
            pltpu.VMEM((512, 512), BF16),
            pltpu.VMEM((512, 512), BF16),
            pltpu.VMEM((512, 1024), BF16),
            pltpu.VMEM((SHARD, 1024), BF16),
            pltpu.VMEM((512, 512), BF16),
            pltpu.VMEM((512, 512), BF16),
            pltpu.VMEM((512, 1024), BF16),
            pltpu.SemaphoreType.DMA((4,)),
            pltpu.SemaphoreType.DMA((4,)),
            pltpu.VMEM((NZ, 256, 1024), BF16),
            pltpu.VMEM((3, 8, 256, 512), BF16),
            pltpu.VMEM((256, 512), BF16),
            pltpu.VMEM((NZ, 256, 1024), BF16),
            pltpu.VMEM((2, 512, 512), BF16),
            pltpu.VMEM((2, 512, 512), BF16),
            pltpu.VMEM((3, 8, 256, 512), BF16),
            pltpu.VMEM((2, 512, 512), F32),
            pltpu.VMEM((2, 512, 512), F32),
            pltpu.VMEM((2, 512, 512), BF16),
            pltpu.VMEM((2, 512, 512), BF16),
            pltpu.VMEM((15, PCUT, 1024), BF16),
            pltpu.VMEM((15, SHARD - PCUT, 1024), BF16),
            pltpu.VMEM((3, 4, 256, 512), BF16),
            pltpu.VMEM((3, 6, 128, 512), BF16),
            pltpu.VMEM((2, 256, 512), BF16),
            pltpu.SemaphoreType.DMA((128,)),
            pltpu.SemaphoreType.DMA((128,)),
        ],
        compiler_params=pltpu.CompilerParams(
            collective_id=0, has_side_effects=True, vmem_limit_bytes=58 * 2**20
        ),
        cost_estimate=pl.CostEstimate(flops=12 * 2**30, bytes_accessed=8 * 2**20, transcendentals=2**19),
    )(grad_out, gate_pre, up_pre, weight, block_mask)
    return pl.pallas_call(
        hand_on,
        out_shape=[jax.ShapeDtypeStruct(r.shape, r.dtype) for r in results],
        in_specs=[anywhere] * 4,
        out_specs=[anywhere] * 4,
        scratch_shapes=[pltpu.VMEM(r.shape, r.dtype) for r in results] + [pltpu.SemaphoreType.DMA((2, 4))],
    )(*results)


def solution(mesh):
    placed = (P("col", "row"), P("col", "row"), P("row", "col"), P("row", "col"), P("row", "col"))
    return jax.shard_map(
        shards,
        mesh=mesh,
        in_specs=placed,
        out_specs=(P("row", "col"), P("col", "row"), P("col", "row"), P("row", "col")),
        check_vma=False,
    )
```

```python
import jax
import jax.numpy as jnp
from jax import lax
from jax.experimental import pallas as pl
from jax.experimental.pallas import tpu as pltpu
from jax.sharding import PartitionSpec as P

NZ, NX, NY = 8, 4, 4
SHARD = 128
GCUT, PCUT = 32, 48
MESH = pl.DeviceIdType.MESH
F32 = jnp.float32
BF16 = jnp.bfloat16


class Slots:
    def __init__(self):
        self.known = {}

    def __call__(self, *key):
        return self.known.setdefault(key, len(self.known))


def dot(a, b, a_dim, b_dim):
    return lax.dot_general(a, b, (((a_dim,), (b_dim,)), ((), ())), preferred_element_type=F32)


def tile(n, size):
    return pl.ds(pl.multiple_of(n * size, size), size)


def kernel(
    grad_in, gate_in, up_in, weight_in, mask_ref,
    out_to, dgate_to, dup_to, dweight_to,
    gate_ref, up_ref, weight_ref, out_ref, dgate_ref, dup_ref, dweight_ref, in_sem, out_sem,
    gall, hall, hx, part, wm, wo, dpart, acc, accx, wsend, wrecv,
    land_a, land_b, land_s, land_y, land_x,
    send_sem, recv_sem,
):
    row, col = lax.axis_index("row"), lax.axis_index("col")
    z, x = row // NX, row % NX
    y, core = col // 2, col % 2
    parity = x % 2
    near = 1 - 2 * parity

    def zi(o):
        return lax.rem(z + (o + NZ), NZ)

    def xi(d):
        return lax.rem(x + (d + NX), NX)

    def yi(d):
        return lax.rem(y + (d + NY), NY)

    def zdev(d):
        return (zi(d) * NX + x, col)

    def xdev(d):
        return (z * NX + xi(d), col)

    def ydev(d):
        return (row, yi(d) * 2 + core)

    sibling = (row, y * 2 + (1 - core))
    mates = (xdev(near), xdev(-near))
    across = xdev(2)

    sems, slot_a, slot_b = Slots(), Slots(), Slots()
    sends = []

    def send(src, dst, dev, *key):
        copy = pltpu.make_async_remote_copy(
            src_ref=src, dst_ref=dst, send_sem=send_sem.at[len(sends)],
            recv_sem=recv_sem.at[sems(*key)], device_id=dev, device_id_type=MESH,
        )
        copy.start()
        sends.append(copy)

    def arrive(dst, *key):
        pltpu.make_async_remote_copy(
            src_ref=dst, dst_ref=dst, send_sem=send_sem.at[0],
            recv_sem=recv_sem.at[sems(*key)], device_id=sibling, device_id_type=MESH,
        ).wait_recv()

    def add(dst, rows, *terms):
        @pl.loop(0, rows // 16)
        def _(i):
            at = tile(i, 16)
            total = terms[0].at[at, :][...].astype(F32)
            for term in terms[1:]:
                total = total + term.at[at, :][...].astype(F32)
            dst.at[at, :][...] = total.astype(BF16)

    barrier = pltpu.get_barrier_semaphore()
    for dev in (zdev(1), zdev(-1), xdev(1), xdev(-1), across, ydev(1), ydev(-1), sibling):
        pl.semaphore_signal(barrier, inc=1, device_id=dev, device_id_type=MESH)

    mine, other = x // 2, 1 - x // 2
    taken = {}
    for n, (name, src, dst) in enumerate((
        ("grad", grad_in, gall.at[z, pl.ds(pl.multiple_of(mine * SHARD, SHARD), SHARD), :]),
        ("gate", gate_in, gate_ref),
        ("up", up_in, up_ref),
        ("weight", weight_in, weight_ref),
    )):
        taken[name] = pltpu.make_async_copy(src, dst, in_sem.at[n])
        taken[name].start()
    results = ((out_ref, out_to), (dgate_ref, dgate_to), (dup_ref, dup_to), (dweight_ref, dweight_to))
    given = [pltpu.make_async_copy(src, dst, out_sem.at[n]) for n, (src, dst) in enumerate(results)]

    def hidden_into(dst, which):
        for j in (0, 1):
            @pl.loop(0, 4)
            def _(i):
                at = pl.ds(pl.multiple_of((which + 2 * j) * SHARD + i * 32, 32), 32)
                g = gate_ref[at, :].astype(F32)
                u = up_ref[at, :].astype(F32)
                dst.at[pl.ds(pl.multiple_of(j * SHARD + i * 32, 32), 32), :][...] = (
                    g * jax.nn.sigmoid(g) * u
                ).astype(BF16)

    pl.semaphore_wait(barrier, 8)
    taken["grad"].wait()

    def rows(buf, o, e, start, size):
        return buf.at[zi(o), pl.ds(pl.multiple_of((other if e else mine) * SHARD + start, 16), size), :]

    def ga(o, e):
        return rows(gall, o, e, 0, GCUT)

    def gb(o, e):
        return rows(gall, o, e, GCUT, SHARD - GCUT)

    def hid(f, dy, h=None):
        at = slice(None) if h is None else pl.ds(h * 128, 128)
        return hall.at[f, yi(dy) * 2 + core, at, :]

    def hid_sibling(f, dy):
        return hall.at[f, yi(dy) * 2 + (1 - core)]

    def az_next(o):
        if o <= 0 and o > -4:
            send(ga(o, 0), ga(o, 0), zdev(1), "gaz", o - 1)
        if o >= 0 and o < 3:
            send(ga(o, 0), ga(o, 0), zdev(-1), "gaz", o + 1)

    def ax_send(o):
        send(ga(o, 0), ga(o, 0), across, "gax", o)

    def az(*offsets):
        for o in offsets:
            arrive(ga(o, 0), "gaz", o)
            az_next(o)
            ax_send(o)

    def ax(*offsets):
        for o in offsets:
            arrive(ga(o, 1), "gax", o)

    def bz_first(e):
        send(gb(0, e), gb(0, e), zdev(1), "gbz", e, -1)
        send(gb(0, e), gb(0, e), zdev(-1), "gbz", e, 1)

    def bx():
        arrive(gb(0, 1), "gbx")
        bz_first(1)

    def bzo(o, e):
        low, high = (-4, 3) if e == 0 else (-3, 4)
        arrive(gb(o, e), "gbz", e, o)
        if o < 0 and o > low:
            send(gb(o, e), gb(o, e), zdev(1), "gbz", e, o - 1)
        if o > 0 and o < high:
            send(gb(o, e), gb(o, e), zdev(-1), "gbz", e, o + 1)

    def hx_out():
        for s in (0, 1):
            send(hx, hall.at[1 + s, col], mates[s], "hx", s)

    def hx_in():
        for s in (0, 1):
            arrive(hall.at[1 + s, col], "hx", s)

    def h0(f):
        for h in (0, 1):
            send(hid(f, 0, h), hid(f, 0, h), ydev(1), "hy", f, -1, h)
            send(hid(f, 0, 1 - h), hid(f, 0, 1 - h), ydev(-1), "hy", f, 1, 1 - h)
        send(hid(f, 0), hid(f, 0), sibling, "hs", f, 0)

    def h1(f):
        arrive(hid(f, -1, 0), "hy", f, -1, 0)
        send(hid(f, -1, 0), hid(f, -1, 0), ydev(1), "hy2", f, 0)
        arrive(hid(f, 1, 1), "hy", f, 1, 1)
        send(hid(f, 1, 1), hid(f, 1, 1), ydev(-1), "hy2", f, 1)

    def h2(f):
        arrive(hid(f, -1, 1), "hy", f, -1, 1)
        send(hid(f, -1), hid(f, -1), sibling, "hs", f, -1)
        arrive(hid(f, 1, 0), "hy", f, 1, 0)
        send(hid(f, 1), hid(f, 1), sibling, "hs", f, 1)

    def h3(f):
        arrive(hid(f, 2, 0), "hy2", f, 0)
        arrive(hid(f, 2, 1), "hy2", f, 1)
        send(hid(f, 2), hid(f, 2), sibling, "hs", f, 2)

    def h4(f):
        for dy in (0, -1, 1, 2):
            arrive(hid_sibling(f, dy), "hs", f, dy)

    def mm_part(o):
        block = zi(o)
        for s in (0, 1):
            part[block, :, pl.ds(s * 512, 512)] = (
                dot(hall[0, block], wm[s], 1, 0) + dot(hall[1 + s, block], wo[s], 1, 0)
            ).astype(BF16)

    def mm_dpart(f, block):
        first, second = gall[block, :, pl.ds(0, 512)], gall[block, :, pl.ds(512, 512)]
        if f == 0:
            product = dot(first, wm[0], 1, 1) + dot(second, wm[1], 1, 1)
        else:
            product = dot((first, second)[f - 1], wo[f - 1], 1, 1)
        dpart[f, block] = product.astype(BF16)

    def mm_sum(dst, f, s):
        for k in (0, 1):
            blocks = pl.ds(4 * k, 4)
            product = dot(
                hall[f, blocks].reshape(1024, 512), gall[blocks, :, pl.ds(s * 512, 512)].reshape(1024, 512), 0, 0
            )
            dst[...] = product if k == 0 else dst[...] + product

    def mm_mate(s):
        mm_sum(accx.at[s], 1 + s, s)

    def mm_own(s):
        mm_sum(acc.at[s], 0, s)

    def pa(o, e):
        return rows(part, o, e, 0, PCUT)

    def pb(o, e):
        return rows(part, o, e, PCUT, SHARD - PCUT)

    def la(*key):
        return land_a.at[slot_a(*key)]

    def lb(*key):
        return land_b.at[slot_b(*key)]

    def xs(o):
        send(pa(o, 1), la("px", o), across, "px", o)

    def zf(o):
        sides = []
        if 0 <= o < 3:
            sides.append(-1)
        if -4 < o <= 0:
            sides.append(1)
        held = la("px", o)
        arrive(held, "px", o)
        terms = [pa(o, 0), held]
        for side in sides:
            arrive(la("pz", o, side), "pz", o, side)
            terms.append(la("pz", o, side))
        if o == 0:
            add(out_ref.at[pl.ds(0, PCUT), :], PCUT, *terms)
            return
        add(held, PCUT, *terms)
        if o == 4:
            send(held, la("pz", -3, 1), zdev(-1), "pz", -3, 1)
        elif o > 0:
            send(held, la("pz", o - 1, -1), zdev(1), "pz", o - 1, -1)
        else:
            send(held, la("pz", o + 1, 1), zdev(-1), "pz", o + 1, 1)

    def rz(o, e):
        sides = []
        if 0 <= o < 4 and not (o == 3 and e == 1):
            sides.append(-1)
        if -4 < o <= 0 and not (o == -3 and e == 0):
            sides.append(1)
        terms = [pb(o, e)]
        for side in sides:
            held = lb("pbz", e, o, side)
            arrive(held, "pbz", e, o, side)
            terms.append(held)
        src = terms[-1]
        if len(terms) > 1:
            add(src, SHARD - PCUT, *terms)
        if o == 4:
            if e == 0:
                send(src, lb("pbz", e, 3, -1), zdev(1), "pbz", e, 3, -1)
            else:
                send(src, lb("pbz", e, -3, 1), zdev(-1), "pbz", e, -3, 1)
        elif o > 0:
            send(src, lb("pbz", e, o - 1, -1), zdev(1), "pbz", e, o - 1, -1)
        elif o < 0:
            send(src, lb("pbz", e, o + 1, 1), zdev(-1), "pbz", e, o + 1, 1)
        elif e == 1:
            send(src, lb("pbx"), across, "pbx")

    def bf():
        held = lb("pbx")
        arrive(held, "pbx")
        add(out_ref.at[pl.ds(PCUT, SHARD - PCUT), :], SHARD - PCUT, lb("pbz", 0, 0, 1), held)

    S = {2: 0, -1: 1, 1: 2, 0: 3}
    Y = {("m", -1): 0, ("m", 1): 1, (-1, 0): 2, (-1, 1): 3, (1, 0): 4, (1, 1): 5}
    DYS = (2, -1, 1, 0)

    def own(dy):
        return yi(dy) * 2 + core

    def dhalf(f, dy, h):
        return dpart.at[f, own(dy), pl.ds(h * 128, 128), :]

    def ly(f, *key):
        return land_y.at[f, Y[key]]

    def dsib(f):
        for dy in DYS:
            block = yi(dy) * 2 + (1 - core)
            mm_dpart(f, block)
            send(dpart.at[f, block], land_s.at[f, S[dy]], sibling, "ds", f, dy)

    def down(f):
        for dy in DYS:
            mm_dpart(f, own(dy))

    def dadd(f):
        for dy in DYS:
            held = land_s.at[f, S[dy]]
            arrive(held, "ds", f, dy)
            here = dpart.at[f, own(dy)]
            add(here, 256, here, held)
            if dy == 2:
                send(dhalf(f, 2, 0), ly(f, "m", -1), ydev(1), "dym", f, -1)
                send(dhalf(f, 2, 1), ly(f, "m", 1), ydev(-1), "dym", f, 1)
            if dy == 1:
                send(dhalf(f, 1, 1), ly(f, -1, 1), ydev(1), "dyf", f, -1, 1)
            if dy == -1:
                send(dhalf(f, -1, 0), ly(f, 1, 0), ydev(-1), "dyf", f, 1, 0)

    def dmid(f):
        for side, h in ((-1, 0), (1, 1)):
            held = ly(f, "m", side)
            arrive(held, "dym", f, side)
            add(held, 128, held, dhalf(f, -side, h))
            send(held, ly(f, side, h), ydev(-side), "dyf", f, side, h)

    def dend(f):
        for h in (1, 0):
            for side in (-1, 1):
                arrive(ly(f, side, h), "dyf", f, side, h)

    def dmate(f):
        dend(f)
        for h in (0, 1):
            add(dhalf(f, 0, h), 128, dhalf(f, 0, h), ly(f, -1, h), ly(f, 1, h))
        send(dpart.at[f, own(0)], land_x.at[f - 1], mates[f - 1], "dx", f)

    def grads(which, j, *terms):
        @pl.loop(0, 4)
        def _(i):
            at = tile(i, 32)
            rows = pl.ds(pl.multiple_of((which + 2 * j) * SHARD + i * 32, 32), 32)
            dh = terms[0].at[at, :][...].astype(F32)
            for term in terms[1:]:
                dh = dh + term.at[at, :][...].astype(F32)
            g = gate_ref[rows, :].astype(F32)
            u = up_ref[rows, :].astype(F32)
            sig = jax.nn.sigmoid(g)
            dup_ref[rows, :] = (dh * g * sig).astype(BF16)
            dgate_ref[rows, :] = (dh * u * sig * (1.0 + g * (1.0 - sig))).astype(BF16)

    def grads_own():
        dend(0)
        for h in (0, 1):
            grads(parity, h, dhalf(0, 0, h), ly(0, -1, h), ly(0, 1, h))

    def grads_mates():
        for f in (1, 2):
            arrive(land_x.at[f - 1], "dx", f)
        for h in (0, 1):
            at = pl.ds(h * 128, 128)
            grads(1 - parity, h, land_x.at[0, at, :], land_x.at[1, at, :])

    def keep(i, j):
        return mask_ref[i, j].astype(F32)

    def mask_weights():
        @pl.loop(0, 4)
        def _(i):
            for j in range(8):
                wm[j // 4, tile(i, 128), pl.ds(j % 4 * 128, 128)] = (
                    weight_ref[tile(i, 128), pl.ds(j * 128, 128)].astype(F32) * keep(i, j)
                ).astype(BF16)

    def weights_out():
        for s in (0, 1):
            send(wm.at[s], wo.at[s], mates[s], "w", s)

    def weights_in():
        for s in (0, 1):
            arrive(wo.at[s], "w", s)

    def dweights_out():
        for s in (0, 1):
            @pl.loop(0, 16)
            def _(i):
                wsend[s, tile(i, 32), :] = accx[s, tile(i, 32), :].astype(BF16)
            send(wsend.at[s], wrecv.at[s], mates[s], "dw", s)

    def dweights_in():
        for s in (0, 1):
            arrive(wrecv.at[s], "dw", s)

        @pl.loop(0, 4)
        def _(i):
            for j in range(8):
                at = (j // 4, tile(i, 128), pl.ds(j % 4 * 128, 128))
                dweight_ref[tile(i, 128), pl.ds(j * 128, 128)] = (
                    (acc[at] + wrecv[at].astype(F32)) * keep(i, j)
                ).astype(BF16)

    az_next(0)
    send(gb(0, 0), gb(0, 0), across, "gbx")
    bz_first(0)
    taken["gate"].wait()
    taken["up"].wait()
    hidden_into(hx, 1 - parity)
    hx_out()
    hidden_into(hall.at[0, col], parity)
    h0(0)
    ax_send(0)
    taken["weight"].wait()
    mask_weights()
    az(-1)
    az(1)
    bx()
    weights_out()
    h1(0)
    bzo(1, 0)
    bzo(-1, 0)
    az(2)
    az(-2)
    h2(0)
    hx_in()
    h0(1)
    h0(2)
    h3(0)
    ax(0)
    bzo(1, 1)
    bzo(-1, 1)
    ax(-1)
    h4(0)
    ax(1)
    bzo(2, 0)
    bzo(-2, 0)
    h1(1)
    az(3)
    az(-3)
    h2(1)
    bzo(-2, 1)
    bzo(2, 1)
    h1(2)
    h2(2)
    bzo(3, 0)
    bzo(-3, 0)
    weights_in()
    az(-4)
    ax(2)
    h3(1)
    ax(-2)
    h4(1)
    bzo(3, 1)
    ax(3)
    h3(2)
    bzo(-3, 1)
    ax(-3)
    h4(2)
    mm_part(-2)
    ax(-4)
    mm_part(4)
    rz(4, 0)
    xs(-2)
    xs(4)
    mm_part(-3)
    mm_part(-1)
    xs(-1)
    rz(4, 1)
    mm_part(0)
    bzo(-4, 0)
    mm_part(3)
    xs(3)
    xs(0)
    bzo(4, 1)
    dsib(1)
    down(1)
    dsib(2)
    mm_mate(1)
    zf(4)
    dadd(1)
    rz(-3, 1)
    rz(3, 1)
    mm_part(1)
    xs(1)
    rz(3, 0)
    rz(-3, 0)
    down(2)
    dadd(2)
    xs(-3)
    mm_part(2)
    xs(2)
    mm_mate(0)
    dweights_out()
    dmid(1)
    rz(-2, 1)
    rz(2, 1)
    zf(3)
    dsib(0)
    zf(-3)
    down(0)
    rz(2, 0)
    dmid(2)
    rz(-2, 0)
    mm_own(1)
    dadd(0)
    rz(1, 1)
    rz(-1, 1)
    mm_own(0)
    zf(2)
    zf(-2)
    dmate(1)
    dmate(2)
    rz(-1, 0)
    rz(1, 0)
    dmid(0)
    dweights_in()
    given[3].start()
    rz(0, 1)
    zf(-1)
    zf(1)
    grads_own()
    grads_mates()
    given[1].start()
    given[2].start()
    rz(0, 0)
    zf(0)
    bf()
    given[0].start()

    for copy in sends:
        copy.wait_send()
    for copy in given:
        copy.wait()


def hand_on(*refs):
    sources, targets, held, sem = refs[:4], refs[4:8], refs[8:12], refs[12]
    pieces = [(3, 0), (3, 128), (3, 256), (3, 384), (1, 0), (1, 256), (2, 0), (2, 256), (0, 0)]
    sizes = {0: SHARD, 1: 256, 2: 256, 3: 128}
    ins, outs = [], []
    for n, (which, start) in enumerate(pieces):
        at = pl.ds(start, sizes[which])
        middle = held[which].at[at, :]
        ins.append(pltpu.make_async_copy(sources[which].at[at, :], middle, sem.at[0, n]))
        outs.append(pltpu.make_async_copy(middle, targets[which].at[at, :], sem.at[1, n]))
    for copy in ins:
        copy.start()
    for first, then in zip(ins, outs):
        first.wait()
        then.start()
    for copy in outs:
        copy.wait()


def shards(gate_pre, up_pre, weight, block_mask, grad_out):
    anywhere = pl.BlockSpec(memory_space=pl.ANY)
    results = pl.pallas_call(
        kernel,
        out_shape=(
            jax.ShapeDtypeStruct((SHARD, 1024), BF16),
            jax.ShapeDtypeStruct((512, 512), BF16),
            jax.ShapeDtypeStruct((512, 512), BF16),
            jax.ShapeDtypeStruct((512, 1024), BF16),
        ),
        in_specs=[anywhere] * 4 + [pl.BlockSpec(memory_space=pltpu.SMEM)],
        out_specs=[anywhere] * 4,
        scratch_shapes=[
            pltpu.VMEM((512, 512), BF16),
            pltpu.VMEM((512, 512), BF16),
            pltpu.VMEM((512, 1024), BF16),
            pltpu.VMEM((SHARD, 1024), BF16),
            pltpu.VMEM((512, 512), BF16),
            pltpu.VMEM((512, 512), BF16),
            pltpu.VMEM((512, 1024), BF16),
            pltpu.SemaphoreType.DMA((4,)),
            pltpu.SemaphoreType.DMA((4,)),
            pltpu.VMEM((NZ, 256, 1024), BF16),
            pltpu.VMEM((3, 8, 256, 512), BF16),
            pltpu.VMEM((256, 512), BF16),
            pltpu.VMEM((NZ, 256, 1024), BF16),
            pltpu.VMEM((2, 512, 512), BF16),
            pltpu.VMEM((2, 512, 512), BF16),
            pltpu.VMEM((3, 8, 256, 512), BF16),
            pltpu.VMEM((2, 512, 512), F32),
            pltpu.VMEM((2, 512, 512), F32),
            pltpu.VMEM((2, 512, 512), BF16),
            pltpu.VMEM((2, 512, 512), BF16),
            pltpu.VMEM((15, PCUT, 1024), BF16),
            pltpu.VMEM((15, SHARD - PCUT, 1024), BF16),
            pltpu.VMEM((3, 4, 256, 512), BF16),
            pltpu.VMEM((3, 6, 128, 512), BF16),
            pltpu.VMEM((2, 256, 512), BF16),
            pltpu.SemaphoreType.DMA((128,)),
            pltpu.SemaphoreType.DMA((128,)),
        ],
        compiler_params=pltpu.CompilerParams(
            collective_id=0, has_side_effects=True, vmem_limit_bytes=58 * 2**20
        ),
        cost_estimate=pl.CostEstimate(flops=12 * 2**30, bytes_accessed=8 * 2**20, transcendentals=2**19),
    )(grad_out, gate_pre, up_pre, weight, block_mask)
    return pl.pallas_call(
        hand_on,
        out_shape=[jax.ShapeDtypeStruct(r.shape, r.dtype) for r in results],
        in_specs=[anywhere] * 4,
        out_specs=[anywhere] * 4,
        scratch_shapes=[pltpu.VMEM(r.shape, r.dtype) for r in results] + [pltpu.SemaphoreType.DMA((2, 9))],
    )(*results)


def solution(mesh):
    placed = (P("col", "row"), P("col", "row"), P("row", "col"), P("row", "col"), P("row", "col"))
    return jax.shard_map(
        shards,
        mesh=mesh,
        in_specs=placed,
        out_specs=(P("row", "col"), P("col", "row"), P("col", "row"), P("row", "col")),
        check_vma=False,
    )
```
